256 devices in a mesh: dp: 16 (over z, y_hi), tensor: 16 (over x, y_lo, core).
Axes of the slice: x: 4, y: 4 (y_hi: 2, y_lo: 2; y = y_hi * 2 + y_lo), z: 8, core: 2. Of those that a mesh axis runs over, the one named last changes fastest.
Arguments:
- inputs: bfloat16 [4096, 5120], P('dp'), may hold values from -6 to 6
- upstream: bfloat16 [4096, 5120], P('dp'), may hold values from -6 to 6
- w_in: bfloat16 [5120, 10240], P('dp', 'tensor'), may hold values from -0.125 to 0.125
- bias_in: bfloat16 [10240], P('tensor'), may hold values from -3 to 3
- w_out: bfloat16 [10240, 5120], P('tensor', 'dp'), may hold values from -0.0625 to 0.0625
Outputs:
- grad_inputs: bfloat16 [4096, 5120], P('dp', 'tensor')
- grad_w_in: float32 [5120, 10240], P('dp', 'tensor')
- grad_w_out: float32 [10240, 5120], P('tensor', 'dp')
The draws below stay inside these ranges and needn't reach their ends.
All inputs are finite; a program needn't handle non-finite values.
Results may differ from the reference program's by a relative error of at most 0.022.
Values may be sent and summed in bfloat16 or wider, within the bound.
A program may use at most 128 MiB of HBM per device.

```python
import math
import jax
import jax.numpy as jnp
from jax import lax

D = 5120
FF = 10240
TOK_DEV = 256
TOKENS = 4096
N_DP = 16
N_TENSOR = 16


def raised(values, own_key, source, target, parts, factor):
    owner, partner = [(jnp.arange(values.shape[axis_at]) // (values.shape[axis_at] // parts)).reshape([-1 if axis == axis_at else 1 for axis in range(values.ndim)]) for axis_at in (source, target)]
    chosen = jax.random.permutation(own_key, parts)[partner]
    strong = (owner == chosen) | (owner == (partner + parts // 2) % parts)
    return jnp.where(strong, factor * values, values)


def block_scale(rng, dims, split, low, top_value):
    level = 1.0
    for axis_at, shards_of in split:
        steps = jax.random.uniform(jax.random.fold_in(jax.random.fold_in(rng, 6), axis_at), (shards_of,), jnp.float32, low / len(split), top_value / len(split))
        level = level * jnp.repeat(jnp.exp(steps), dims[axis_at] // shards_of).reshape((-1,) + (1,) * (len(dims) - 1 - axis_at))
    return level


def normal_values(rng, shape, width, bound, shards=(), held_as=jnp.bfloat16):
    result = width * jax.random.normal(rng, shape, jnp.float32)
    if shards:
        result = result * block_scale(rng, shape, shards, -0.22, 0.18)
    return jnp.clip(result, -bound, bound).astype(held_as)


def gaussian_with(stream_key, shape, width, limit, pieces, heavy, kind=jnp.bfloat16):
    entries = width * jax.random.normal(stream_key, shape, jnp.float32)
    if pieces:
        entries = entries * block_scale(stream_key, shape, pieces, -0.22, 0.18)
    return jnp.clip(raised(entries, jax.random.fold_in(stream_key, 3), *heavy), -limit, limit).astype(kind)


def setup_inputs(seed: int = 0) -> dict:
    keys = jax.random.split(jax.random.key(seed), 6)
    inputs = gaussian_with(keys[0], (TOKENS, D), 1.0, 6.0, ((0, 16),), (0, 1, 16, 2.0))
    upstream = gaussian_with(keys[1], (TOKENS, D), 1.0, 6.0, ((0, 16),), (0, 1, 16, 2.0))
    w_in = gaussian_with(keys[2], (D, FF), D ** -0.5, 0.125, ((0, 16), (1, 16)), (1, 0, 16, 2.0))
    bias_in = normal_values(keys[3], (FF,), 0.5, 3.0, ((0, 16),))
    w_out = normal_values(keys[4], (FF, D), FF ** -0.5, 0.0625, ((0, 16), (1, 16)))
    return {"inputs": inputs, "upstream": upstream, "w_in": w_in, "bias_in": bias_in, "w_out": w_out}


root_half = 0.7071067811865476
inv_root_two_pi = 0.3989422804014327

def gelu_pair(pre_act):
    normal_cdf = 0.5 * (1.0 + lax.erf(pre_act * root_half))
    gelu_value = pre_act * normal_cdf
    gelu_slope = normal_cdf + pre_act * jnp.exp(-0.5 * pre_act * pre_act) * inv_root_two_pi
    return (gelu_value, gelu_slope)

def rounded_add(running, term):
    narrow = lax.optimization_barrier(term.astype(jnp.bfloat16))
    return running + narrow.astype(jnp.float32)

def reference(inputs, upstream, w_in, bias_in, w_out):
    pre_act = jnp.dot(inputs, w_in, preferred_element_type=jnp.float32) + bias_in.astype(jnp.float32)
    gelu_value, gelu_slope = gelu_pair(pre_act)
    activated = gelu_value.astype(jnp.bfloat16)
    grad_act = lax.dot_general(upstream, w_out, (((1,), (1,)), ((), ())), preferred_element_type=jnp.float32)
    grad_pre = (grad_act * gelu_slope).astype(jnp.bfloat16)
    grad_scale = 1.0 / math.sqrt(TOKENS)
    group = FF // N_TENSOR

    def add_inputs(running, index):
        offset = (index * group).astype(jnp.int32)
        grad_cols = lax.dynamic_slice_in_dim(grad_pre, offset, group, 1)
        weight_cols = lax.dynamic_slice_in_dim(w_in, offset, group, 1)
        term = lax.dot_general(grad_cols, weight_cols, (((1,), (1,)), ((), ())), preferred_element_type=jnp.float32)
        return (rounded_add(running, term), None)
    grad_x, _ = lax.scan(add_inputs, jnp.zeros((TOKENS, D), jnp.float32), jnp.arange(N_TENSOR, dtype=jnp.int32))
    grad_inputs = grad_x.astype(jnp.bfloat16)

    def add_weights(carry, index):
        first, second = carry
        offset = (index * TOK_DEV).astype(jnp.int32)
        in_rows = lax.dynamic_slice_in_dim(inputs, offset, TOK_DEV, 0)
        grad_rows = lax.dynamic_slice_in_dim(grad_pre, offset, TOK_DEV, 0)
        act_rows = lax.dynamic_slice_in_dim(activated, offset, TOK_DEV, 0)
        up_rows = lax.dynamic_slice_in_dim(upstream, offset, TOK_DEV, 0)
        term_in = lax.dot_general(in_rows, grad_rows, (((0,), (0,)), ((), ())), preferred_element_type=jnp.float32) * grad_scale
        term_out = lax.dot_general(act_rows, up_rows, (((0,), (0,)), ((), ())), preferred_element_type=jnp.float32) * grad_scale
        return ((rounded_add(first, term_in), rounded_add(second, term_out)), None)
    start_pair = (jnp.zeros((D, FF), jnp.float32), jnp.zeros((FF, D), jnp.float32))
    (grad_w_in, grad_w_out), _ = lax.scan(add_weights, start_pair, jnp.arange(N_DP, dtype=jnp.int32))
    return (grad_inputs, grad_w_in, grad_w_out)
```

```python
import math

import jax
import jax.numpy as jnp
from jax import lax
from jax.experimental import pallas as pl
from jax.experimental.pallas import tpu as pltpu
from jax.sharding import PartitionSpec as P

MESH = pl.DeviceIdType.MESH
ROOT_HALF = 0.7071067811865476
INV_ROOT_TWO_PI = 0.3989422804014327
BF16 = jnp.bfloat16
F32 = jnp.float32

NZ = 8
NT = 8
ROWS = 256
SH = 320
HF = SH // 2
FC = 640
A = pl.ds(0, HF)
B = pl.ds(HF, HF)
FULL = pl.ds(0, SH)

TN = (((0,), (0,)), ((), ()))
NN = (((1,), (0,)), ((), ()))
NT_DIMS = (((1,), (1,)), ((), ()))


def dot(lhs, rhs, dims):
    return lax.dot_general(lhs, rhs, dims, preferred_element_type=F32)


def kernel(
    scale, x_hbm, dy_hbm, win_hbm, wout_hbm, bias_ref,
    dx_out, dwin_out, dwout_out,
    xv, dyv, wov, wt, xt, dyt, wi, wo,
    pre, pre_in, act, ga, ga_in, gp, slope,
    term_o, term_i, rin_o, rin_i, lin_o, lin_i, own_o, own_i,
    dxs, dxr, bias_in,
    ld_sem, sw_s, sw_r, ag_s, ag_r, ex_s, ex_r, core_s, core_r,
    rs_s, rs_r, own_s, own_r, dx_s, dx_r,
):
    dp = lax.axis_index("dp")
    tn = lax.axis_index("tensor")
    z, a = lax.div(dp, 2), lax.rem(dp, 2)
    t2, b = lax.div(tn, 2), lax.rem(tn, 2)
    xpar = lax.rem(lax.div(t2, 2), 2)
    ypar = lax.rem(t2, 2)
    same = a == b
    zr, zl = lax.rem(z + 1, NZ), lax.rem(z + NZ - 1, NZ)

    def dev(z_, t_, a_, b_):
        return {"dp": 2 * z_ + a_, "tensor": 2 * t_ + b_}

    right, left = dev(zr, t2, a, b), dev(zl, t2, a, b)
    swap, swap_r, swap_l = dev(z, t2, b, a), dev(zr, t2, b, a), dev(zl, t2, b, a)
    other_core = dev(z, t2, a, 1 - b)
    y_side = dev(z, t2 + 1 - 2 * ypar, 1 - a, b)
    x_side = dev(z, t2 + 2 - 4 * xpar, a, b)

    def rc(src, dst, ss, rs, to):
        return pltpu.make_async_remote_copy(
            src_ref=src, dst_ref=dst, send_sem=ss, recv_sem=rs, device_id=to, device_id_type=MESH
        )

    ld_x = pltpu.make_async_copy(x_hbm, xv, ld_sem.at[0])
    ld_dy = pltpu.make_async_copy(dy_hbm, dyv, ld_sem.at[1])
    ld_wo = pltpu.make_async_copy(wout_hbm, wov, ld_sem.at[2])
    ld_wi = pltpu.make_async_copy(win_hbm, wi.at[0], ld_sem.at[3])
    pl.when(same)(ld_wi.start)
    ld_wo.start()
    ld_x.start()
    ld_dy.start()

    barrier = pltpu.get_barrier_semaphore()

    def greet(to):
        pl.semaphore_signal(barrier, inc=1, device_id=to, device_id_type=MESH)

    plane = [(r, q) for r in range(NT) for q in range(2) if (r, q) != (0, 0)]

    def flip(q):
        return a + q - 2 * a * q

    def plane_dev(r, q):
        return dev(z, lax.rem(t2 + r, NT), flip(q), b)

    greet(right)
    greet(left)
    greet(other_core)
    for r, q in plane:
        greet(plane_dev(r, q))

    @pl.when(jnp.logical_not(same))
    def _():
        greet(swap)
        greet(swap_r)
        greet(swap_l)

    @pl.when(same)
    def _():
        pl.semaphore_wait(barrier, 18)

    @pl.when(jnp.logical_not(same))
    def _():
        pl.semaphore_wait(barrier, 21)

    weights = (wi, wo)

    def ag(w, g, s, rows, part):
        buf = weights[w]
        if g == 0:
            src, dst, to = s - 1, s, right
        else:
            src, dst, to = (NZ + 1 - s) % NZ, NZ - s, left
        i = ((w * 2 + g) * 4 + s - 1) * 2 + part
        return rc(buf.at[src, rows], buf.at[dst, rows], ag_s.at[i], ag_r.at[i], to)

    swap_wi = rc(win_hbm, wi.at[0], sw_s.at[0], sw_r.at[0], swap)
    swap_wo = rc(wt, wo.at[0], sw_s.at[1], sw_r.at[1], swap)

    @pl.when(same)
    def _():
        ld_wi.wait()
        ag(0, 0, 1, FULL, 0).start()
        ag(0, 1, 1, FULL, 0).start()

    @pl.when(jnp.logical_not(same))
    def _():
        swap_wi.start()

    bias_in[0] = jnp.broadcast_to(bias_ref[...].astype(F32), (8, FC))
    bias_cp = rc(bias_in.at[0], bias_in.at[1], core_s.at[2], core_r.at[2], other_core)
    bias_cp.start()

    ld_wo.wait()
    w_t = wov[...].T

    @pl.when(same)
    def _():
        wo[0] = w_t
        ag(1, 0, 1, FULL, 0).start()
        ag(1, 1, 1, FULL, 0).start()

    @pl.when(jnp.logical_not(same))
    def _():
        wt[...] = w_t
        swap_wo.start()

    pairs = ((0, 1), (7, 2), (6, 3), (5, 4))

    def mine(i):
        p, q = pairs[i]
        return p + (q - p) * xpar

    def theirs(i):
        p, q = pairs[i]
        return q + (p - q) * xpar

    def turn(src, dst, d):
        k = lax.rem(z + NZ - d, NZ)
        v = src[:, pl.ds(pl.multiple_of(k * 2 * SH, 128), 2 * SH)].T
        dst[d, a] = jnp.where(b == 0, v[:SH], v[SH:])

    rows_t = (xt, dyt)

    def ex_y(w, i):
        buf, d, m = rows_t[w], mine(i), w * 8 + i
        return rc(buf.at[d, a], buf.at[d, a], ex_s.at[m], ex_r.at[m], y_side)

    def ex_y_in(w, i):
        buf, d, m = rows_t[w], mine(i), w * 8 + i
        return rc(buf.at[d, 1 - a], buf.at[d, 1 - a], ex_s.at[m], ex_r.at[m], y_side)

    def ex_x(w, i):
        buf, d, m = rows_t[w], mine(i), w * 8 + 4 + i
        return rc(buf.at[d, 1 - a], buf.at[d, 1 - a], ex_s.at[m], ex_r.at[m], x_side)

    def ex_x_in(w, i):
        buf, d, m = rows_t[w], theirs(i), w * 8 + 4 + i
        return rc(buf.at[d, 1 - a], buf.at[d, 1 - a], ex_s.at[m], ex_r.at[m], x_side)

    ld_x.wait()
    for i in range(4):
        turn(xv, xt, pairs[i][0])
        turn(xv, xt, pairs[i][1])
        ex_y(0, i).start()

    @pl.when(jnp.logical_not(same))
    def _():
        swap_wi.wait_recv()
        ag(0, 0, 1, FULL, 0).start()
        ag(0, 1, 1, FULL, 0).start()
        swap_wo.wait_recv()
        ag(1, 0, 1, FULL, 0).start()
        ag(1, 1, 1, FULL, 0).start()

    ld_dy.wait()
    for i in range(4):
        turn(dyv, dyt, pairs[i][0])
        turn(dyv, dyt, pairs[i][1])
        ex_y(1, i).start()

    def pass_on(w, i):
        ex_y_in(w, i).wait_recv()
        ex_x(w, i).start()

    def step(w, s, nxt):
        for g in range(2):
            ag(w, g, s, FULL, 0).wait_recv()
            for rows, part in nxt[g]:
                ag(w, g, s + 1, rows, part).start()

    whole = [[(FULL, 0)], [(FULL, 0)]]

    def accumulate(acc, src, w, slots, first=False):
        n = len(slots)

        def body(i, carry):
            j, h = lax.div(i, 2), lax.rem(i, 2)
            d = slots[0] if n == 1 else slots[0] + j * (slots[1] - slots[0])
            acc[h] += dot(src[d, h], w[d], TN)
            return carry

        if first:
            acc[...] = jnp.zeros_like(acc)
        lax.fori_loop(0, 2 * n, body, 0)

    step(0, 1, whole)
    pass_on(0, 0)
    pass_on(0, 1)
    step(1, 1, whole)
    pass_on(0, 2)
    pass_on(0, 3)
    step(0, 2, whole)
    for i in range(2):
        ex_x_in(0, i).wait_recv()
    accumulate(pre, xt, wi, (0,), True)
    accumulate(pre, xt, wi, (1, 7))
    pass_on(1, 0)
    pass_on(1, 1)
    step(1, 2, [[(A, 0), (B, 1)], [(B, 0), (A, 1)]])
    for i in range(2, 4):
        ex_x_in(0, i).wait_recv()
    accumulate(pre, xt, wi, (2, 6))
    pass_on(1, 2)
    pass_on(1, 3)
    step(0, 3, [[(A, 0)], [(B, 0)]])
    accumulate(pre, xt, wi, (3, 5))
    for i in range(4):
        ex_x_in(1, i).wait_recv()
    accumulate(ga, dyt, wo, (0,), True)
    accumulate(ga, dyt, wo, (1, 7))
    accumulate(ga, dyt, wo, (2, 6))
    ag(1, 0, 3, A, 0).wait_recv()
    ag(1, 0, 4, A, 0).start()
    ag(1, 1, 3, B, 0).wait_recv()
    ag(1, 1, 4, B, 0).start()
    ag(0, 0, 4, A, 0).wait_recv()
    ag(0, 1, 4, B, 0).wait_recv()
    accumulate(pre, xt, wi, (4,))
    pre_cp = rc(pre, pre_in, core_s.at[0], core_r.at[0], other_core)
    pre_cp.start()
    bias_cp.wait_recv()
    bias = jnp.where(same, bias_in[0], bias_in[1])[0:1]
    pre_cp.wait_recv()

    def gelu(i, carry):
        h, rows = lax.div(i, 8), pl.ds(pl.multiple_of(lax.rem(i, 8) * 32, 32), 32)
        v = pre[h, rows] + pre_in[h, rows] + bias
        cdf = 0.5 * (1.0 + lax.erf(v * ROOT_HALF))
        act[h, rows] = (v * cdf).astype(BF16)
        slope[h, rows] = cdf + v * jnp.exp(-0.5 * v * v) * INV_ROOT_TWO_PI
        return carry

    lax.fori_loop(0, 16, gelu, 0)

    terms, rins, lins, owns = (term_o, term_i), (rin_o, rin_i), (lin_o, lin_i), (own_o, own_i)

    def make_terms(w, lo, hi):
        src, val, out = (dyt, xt)[w], (act, gp)[w], terms[w]

        def body(i, carry):
            d = lax.rem(4 + lax.div(i + 1, 2) * (2 * lax.rem(i, 2) - 1) + NZ, NZ)
            total = dot(src[d, 0], val[0], NN) + dot(src[d, 1], val[1], NN)
            out[d] = (total * scale).astype(BF16)
            return carry

        lax.fori_loop(lo, hi, body, 0)

    def rs(w, g, e, rows, part):
        buf = terms[w]
        d = NZ - e if g == 0 else e
        to = (right, left)[g] if e > 1 else (swap_r, swap_l)[g]
        dst = (rins, lins)[g][w]
        i = ((w * 2 + g) * 4 + e - 1) * 2 + part
        return rc(buf.at[d, rows], dst.at[e - 1, rows], rs_s.at[i], rs_r.at[i], to)

    def add_in(w, g, e, rows):
        d = NZ - e if g == 0 else e
        came = (rins, lins)[g][w]
        buf = terms[w]
        buf[d, rows] = (buf[d, rows].astype(F32) + came[e, rows].astype(F32)).astype(BF16)

    def hop(w, g, e, rows, part, rows_in=None, part_in=None):
        rs(w, g, e + 1, rows, part if part_in is None else part_in).wait_recv()
        add_in(w, g, e, rows)
        rs(w, g, e, rows, part).start()

    firsts = (A, B)
    seconds = (B, A)

    def own_copy(w):
        i = w
        return rc(terms[w].at[0], owns[w], own_s.at[i], own_r.at[i], swap)

    def own_local(w):
        return pltpu.make_async_copy(terms[w].at[0], owns[w], own_s.at[2 + w])

    def send_own(w):
        @pl.when(same)
        def _():
            own_local(w).start()

        @pl.when(jnp.logical_not(same))
        def _():
            own_copy(w).start()

    def wait_own(w):
        @pl.when(same)
        def _():
            own_local(w).wait()

        @pl.when(jnp.logical_not(same))
        def _():
            own_copy(w).wait()

    make_terms(0, 0, 3)
    for g in range(2):
        rs(0, g, 4, firsts[g], 0).start()
    for g in range(2):
        rs(0, g, 3, seconds[g], 1).start()
    ag(1, 0, 3, B, 1).wait_recv()
    ag(1, 1, 3, A, 1).wait_recv()
    accumulate(ga, dyt, wo, (3, 5))
    ag(1, 0, 4, A, 0).wait_recv()
    ag(1, 1, 4, B, 0).wait_recv()
    accumulate(ga, dyt, wo, (4,))
    ga_cp = rc(ga, ga_in, core_s.at[1], core_r.at[1], other_core)
    ga_cp.start()
    for g in range(2):
        hop(0, g, 3, firsts[g], 0)
    make_terms(0, 3, 8)
    send_own(0)
    ga_cp.wait_recv()

    def grad(i, carry):
        h, rows = lax.div(i, 8), pl.ds(pl.multiple_of(lax.rem(i, 8) * 32, 32), 32)
        gp[h, rows] = ((ga[h, rows] + ga_in[h, rows]) * slope[h, rows]).astype(BF16)
        return carry

    lax.fori_loop(0, 16, grad, 0)
    make_terms(1, 0, 3)
    for g in range(2):
        rs(1, g, 4, firsts[g], 0).start()
    for g in range(2):
        rs(1, g, 3, seconds[g], 1).start()
    make_terms(1, 3, 8)
    send_own(1)

    def dx_body(i, carry):
        d, h = lax.div(i, 2), lax.rem(i, 2)
        dxs[d, h] = dot(wi[d], gp[h], NT_DIMS).astype(BF16)
        return carry

    lax.fori_loop(0, 16, dx_body, 0)

    def dx_cp(r, q):
        d = lax.rem(z + 2 * NZ - lax.rem(t2 + r, NT), NZ)
        m = 2 * r + q
        return rc(dxs.at[d, flip(q)], dxr.at[m], dx_s.at[m], dx_r.at[m], plane_dev(r, q))

    for r, q in plane:
        dx_cp(r, q).start()

    def both_halves(w, e):
        for g in range(2):
            rs(w, g, e + 1, seconds[g], 1).wait_recv()
            rs(w, g, e + 1, firsts[g], 0).wait_recv()
            add_in(w, g, e, FULL)
            rs(w, g, e, FULL, 0).start()

    both_halves(0, 2)
    for g in range(2):
        hop(1, g, 3, firsts[g], 0)
    for g in range(2):
        rs(0, g, 2, FULL, 0).wait_recv()
        add_in(0, g, 1, FULL)
        rs(0, g, 1, FULL, 0).start()
    for part, pick in ((1, seconds), (0, firsts)):
        for g in range(2):
            hop(1, g, 2, pick[g], part)

    for r, q in plane:
        dx_cp(r, q).wait_recv()
    mine_d = lax.rem(z + NZ - t2, NZ)
    total = dxs[mine_d, a].astype(F32)
    for r, q in plane:
        total = total + dxr[2 * r + q].astype(F32)
    dx_out[...] = total.T.astype(BF16)

    for part, pick in ((1, seconds), (0, firsts)):
        for g in range(2):
            hop(1, g, 1, pick[g], part)

    wait_own(0)
    for g in range(2):
        rs(0, g, 1, FULL, 0).wait_recv()
    dw = own_o[...].astype(F32) + rin_o[0].astype(F32) + lin_o[0].astype(F32)
    dwout_out[...] = dw.T

    wait_own(1)
    for part, pick in ((1, seconds), (0, firsts)):
        for g in range(2):
            rs(1, g, 1, pick[g], part).wait_recv()
    dwin_out[...] = own_i[...].astype(F32) + rin_i[0].astype(F32) + lin_i[0].astype(F32)

    @pl.when(jnp.logical_not(same))
    def _():
        swap_wi.wait_send()
        swap_wo.wait_send()

    for w in range(2):
        for g in range(2):
            ag(w, g, 1, FULL, 0).wait_send()
            ag(w, g, 2, FULL, 0).wait_send()
            ag(w, g, 4, firsts[g], 0).wait_send()
        for i in range(4):
            ex_y(w, i).wait_send()
            ex_x(w, i).wait_send()
    for g in range(2):
        ag(0, g, 3, FULL, 0).wait_send()
        ag(1, g, 3, firsts[g], 0).wait_send()
        ag(1, g, 3, seconds[g], 1).wait_send()
    bias_cp.wait_send()
    pre_cp.wait_send()
    ga_cp.wait_send()
    for w in range(2):
        for g in range(2):
            rs(w, g, 4, firsts[g], 0).wait_send()
            rs(w, g, 3, seconds[g], 1).wait_send()
            rs(w, g, 3, firsts[g], 0).wait_send()
    for g in range(2):
        rs(0, g, 2, FULL, 0).wait_send()
        rs(0, g, 1, FULL, 0).wait_send()
        for e in (2, 1):
            rs(1, g, e, seconds[g], 1).wait_send()
            rs(1, g, e, firsts[g], 0).wait_send()
    for r, q in plane:
        dx_cp(r, q).wait_send()


def per_device(inputs, upstream, w_in, bias_in, w_out):
    rows, width = inputs.shape
    scale = 1.0 / math.sqrt(rows * lax.axis_size("dp"))
    any_space = pl.BlockSpec(memory_space=pl.ANY)
    vmem = pl.BlockSpec(memory_space=pltpu.VMEM)
    shard = (SH, FC)
    ring = (NZ,) + shard
    acc = (2, ROWS, FC)
    turned = (NZ, 2, SH, ROWS)
    return pl.pallas_call(
        lambda *refs: kernel(scale, *refs),
        out_shape=(
            jax.ShapeDtypeStruct((ROWS, SH), BF16),
            jax.ShapeDtypeStruct((SH, FC), F32),
            jax.ShapeDtypeStruct((FC, SH), F32),
        ),
        in_specs=[any_space, any_space, any_space, any_space, vmem],
        out_specs=(vmem, vmem, vmem),
        scratch_shapes=[
            pltpu.VMEM((rows, width), BF16),
            pltpu.VMEM((rows, width), BF16),
            pltpu.VMEM((FC, SH), BF16),
            pltpu.VMEM(shard, BF16),
            pltpu.VMEM(turned, BF16),
            pltpu.VMEM(turned, BF16),
            pltpu.VMEM(ring, BF16),
            pltpu.VMEM(ring, BF16),
            pltpu.VMEM(acc, F32),
            pltpu.VMEM(acc, F32),
            pltpu.VMEM(acc, BF16),
            pltpu.VMEM(acc, F32),
            pltpu.VMEM(acc, F32),
            pltpu.VMEM(acc, BF16),
            pltpu.VMEM(acc, F32),
            pltpu.VMEM(ring, BF16),
            pltpu.VMEM(ring, BF16),
            pltpu.VMEM((4,) + shard, BF16),
            pltpu.VMEM((4,) + shard, BF16),
            pltpu.VMEM((4,) + shard, BF16),
            pltpu.VMEM((4,) + shard, BF16),
            pltpu.VMEM(shard, BF16),
            pltpu.VMEM(shard, BF16),
            pltpu.VMEM(turned, BF16),
            pltpu.VMEM((16, SH, ROWS), BF16),
            pltpu.VMEM((2, 8, FC), F32),
            pltpu.SemaphoreType.DMA((4,)),
            pltpu.SemaphoreType.DMA((2,)),
            pltpu.SemaphoreType.DMA((2,)),
            pltpu.SemaphoreType.DMA((32,)),
            pltpu.SemaphoreType.DMA((32,)),
            pltpu.SemaphoreType.DMA((16,)),
            pltpu.SemaphoreType.DMA((16,)),
            pltpu.SemaphoreType.DMA((3,)),
            pltpu.SemaphoreType.DMA((3,)),
            pltpu.SemaphoreType.DMA((32,)),
            pltpu.SemaphoreType.DMA((32,)),
            pltpu.SemaphoreType.DMA((4,)),
            pltpu.SemaphoreType.DMA((4,)),
            pltpu.SemaphoreType.DMA((16,)),
            pltpu.SemaphoreType.DMA((16,)),
        ],
        compiler_params=pltpu.CompilerParams(
            collective_id=0, has_side_effects=True, vmem_limit_bytes=60 * 1024 * 1024
        ),
    )(inputs, upstream, w_in, w_out, bias_in.reshape(1, -1))


def solution(mesh):
    placed = (P("dp", None), P("dp", None), P("dp", "tensor"), P("tensor"), P("tensor", "dp"))
    return jax.shard_map(
        per_device,
        mesh=mesh,
        in_specs=placed,
        out_specs=(P("dp", "tensor"), P("dp", "tensor"), P("tensor", "dp")),
        check_vma=False,
    )
```

```python
import math

import jax
import jax.numpy as jnp
from jax import lax
from jax.experimental import pallas as pl
from jax.experimental.pallas import tpu as pltpu
from jax.sharding import PartitionSpec as P

MESH = pl.DeviceIdType.MESH
ROOT_HALF = 0.7071067811865476
INV_ROOT_TWO_PI = 0.3989422804014327
BF16 = jnp.bfloat16
F32 = jnp.float32

NZ = 8
NT = 8
ROWS = 256
SH = 320
HF = SH // 2
FC = 640
A = pl.ds(0, HF)
B = pl.ds(HF, HF)
FULL = pl.ds(0, SH)

TN = (((0,), (0,)), ((), ()))
NN = (((1,), (0,)), ((), ()))
NT_DIMS = (((1,), (1,)), ((), ()))


def dot(lhs, rhs, dims):
    return lax.dot_general(lhs, rhs, dims, preferred_element_type=F32)


def kernel(
    scale, x_hbm, dy_hbm, win_hbm, wout_hbm, bias_ref,
    dx_out, parts_i, parts_o,
    dx_v, xv, dyv, xt, dyt, wi, wo,
    pre, pre_in, act, ga, ga_in, gp, slope,
    term_o, term_i, rin_o, rin_i, lin_o, lin_i,
    dxs, x_in, ys, y_in, bias_in,
    ld_sem, sw_s, sw_r, ag_s, ag_r, ex_s, ex_r, core_s, core_r,
    rs_s, rs_r, own_s, own_r, dx_s, dx_r,
):
    dp = lax.axis_index("dp")
    tn = lax.axis_index("tensor")
    z, a = lax.div(dp, 2), lax.rem(dp, 2)
    t2, b = lax.div(tn, 2), lax.rem(tn, 2)
    xpar = lax.rem(lax.div(t2, 2), 2)
    ypar = lax.rem(t2, 2)
    same = a == b
    zr, zl = lax.rem(z + 1, NZ), lax.rem(z + NZ - 1, NZ)

    def dev(z_, t_, a_, b_):
        return {"dp": 2 * z_ + a_, "tensor": 2 * t_ + b_}

    right, left = dev(zr, t2, a, b), dev(zl, t2, a, b)
    swap, swap_r, swap_l = dev(z, t2, b, a), dev(zr, t2, b, a), dev(zl, t2, b, a)
    other_core = dev(z, t2, a, 1 - b)
    y_side = dev(z, t2 + 1 - 2 * ypar, 1 - a, b)
    x_side = dev(z, t2 + 2 - 4 * xpar, a, b)

    def rc(src, dst, ss, rs, to):
        return pltpu.make_async_remote_copy(
            src_ref=src, dst_ref=dst, send_sem=ss, recv_sem=rs, device_id=to, device_id_type=MESH
        )

    ld_x = pltpu.make_async_copy(x_hbm, xv, ld_sem.at[0])
    ld_dy = pltpu.make_async_copy(dy_hbm, dyv, ld_sem.at[1])
    ld_wi = pltpu.make_async_copy(win_hbm, wi.at[0], ld_sem.at[2])
    ld_wo = pltpu.make_async_copy(wout_hbm, wo.at[0], ld_sem.at[3])

    @pl.when(same)
    def _():
        ld_wi.start()
        ld_wo.start()

    ld_x.start()
    ld_dy.start()

    put_dx = pltpu.make_async_copy(dx_v, dx_out, ld_sem.at[4])

    barrier = pltpu.get_barrier_semaphore()

    def greet(to):
        pl.semaphore_signal(barrier, inc=1, device_id=to, device_id_type=MESH)

    x_, y_ = lax.div(t2, 2), 2 * a + ypar

    def x_peer(r):
        return lax.rem(x_ + r, 4)

    def y_peer(r):
        yy = lax.rem(y_ + r, 4)
        return lax.rem(yy, 2), lax.div(yy, 2)

    def x_dev(r):
        return dev(z, 2 * x_peer(r) + ypar, a, b)

    def y_dev(r):
        yl, ah = y_peer(r)
        return dev(z, 2 * x_ + yl, ah, b)

    greet(right)
    greet(left)
    greet(other_core)
    for r in (1, 2, 3):
        greet(x_dev(r))
        greet(y_dev(r))

    @pl.when(jnp.logical_not(same))
    def _():
        greet(swap)
        greet(swap_r)
        greet(swap_l)

    @pl.when(same)
    def _():
        pl.semaphore_wait(barrier, 9)

    @pl.when(jnp.logical_not(same))
    def _():
        pl.semaphore_wait(barrier, 12)

    weights = (wi, wo)

    def ag(w, g, s, rows, part):
        buf = weights[w]
        if g == 0:
            src, dst, to = s - 1, s, right
        else:
            src, dst, to = (NZ + 1 - s) % NZ, NZ - s, left
        i = ((w * 2 + g) * 4 + s - 1) * 2 + part
        return rc(buf.at[src, rows], buf.at[dst, rows], ag_s.at[i], ag_r.at[i], to)

    swap_wi = rc(win_hbm, wi.at[0], sw_s.at[0], sw_r.at[0], swap)
    swap_wo = rc(wout_hbm, wo.at[0], sw_s.at[1], sw_r.at[1], swap)

    @pl.when(same)
    def _():
        ld_wi.wait()
        ag(0, 0, 1, FULL, 0).start()
        ag(0, 1, 1, FULL, 0).start()
        ld_wo.wait()
        ag(1, 0, 1, FULL, 0).start()
        ag(1, 1, 1, FULL, 0).start()

    @pl.when(jnp.logical_not(same))
    def _():
        swap_wi.start()
        swap_wo.start()

    bias_in[0] = jnp.broadcast_to(bias_ref[...].astype(F32)[None, :], (8, FC))
    bias_cp = rc(bias_in.at[0], bias_in.at[1], core_s.at[2], core_r.at[2], other_core)
    bias_cp.start()


    pairs = ((0, 1), (7, 2), (6, 3), (5, 4))

    def mine(i):
        p, q = pairs[i]
        return p + (q - p) * xpar

    def theirs(i):
        p, q = pairs[i]
        return q + (p - q) * xpar

    def turn(src, dst, d):
        k = lax.rem(z + NZ - d, NZ)
        v = src[:, pl.ds(pl.multiple_of(k * 2 * SH, 128), 2 * SH)].T
        dst[d, a] = jnp.where(b == 0, v[:SH], v[SH:])

    rows_t = (xt, dyt)

    def ex_y(w, i):
        buf, d, m = rows_t[w], mine(i), w * 8 + i
        return rc(buf.at[d, a], buf.at[d, a], ex_s.at[m], ex_r.at[m], y_side)

    def ex_y_in(w, i):
        buf, d, m = rows_t[w], mine(i), w * 8 + i
        return rc(buf.at[d, 1 - a], buf.at[d, 1 - a], ex_s.at[m], ex_r.at[m], y_side)

    def ex_x(w, i):
        buf, d, m = rows_t[w], mine(i), w * 8 + 4 + i
        return rc(buf.at[d, 1 - a], buf.at[d, 1 - a], ex_s.at[m], ex_r.at[m], x_side)

    def ex_x_in(w, i):
        buf, d, m = rows_t[w], theirs(i), w * 8 + 4 + i
        return rc(buf.at[d, 1 - a], buf.at[d, 1 - a], ex_s.at[m], ex_r.at[m], x_side)

    ld_x.wait()
    for i in range(4):
        turn(xv, xt, pairs[i][0])
        turn(xv, xt, pairs[i][1])
        ex_y(0, i).start()

    @pl.when(jnp.logical_not(same))
    def _():
        swap_wi.wait_recv()
        ag(0, 0, 1, FULL, 0).start()
        ag(0, 1, 1, FULL, 0).start()
        swap_wo.wait_recv()
        ag(1, 0, 1, FULL, 0).start()
        ag(1, 1, 1, FULL, 0).start()

    ld_dy.wait()
    for i in range(4):
        turn(dyv, dyt, pairs[i][0])
        turn(dyv, dyt, pairs[i][1])
        ex_y(1, i).start()

    def pass_on(w, i):
        ex_y_in(w, i).wait_recv()
        ex_x(w, i).start()

    def step(w, s, nxt):
        for g in range(2):
            ag(w, g, s, FULL, 0).wait_recv()
            for rows, part in nxt[g]:
                ag(w, g, s + 1, rows, part).start()

    whole = [[(FULL, 0)], [(FULL, 0)]]

    def accumulate(acc, src, w, slots, first=False):
        n = len(slots)

        def body(i, carry):
            j, h = lax.div(i, 2), lax.rem(i, 2)
            d = slots[0] if n == 1 else slots[0] + j * (slots[1] - slots[0])
            acc[h] += dot(src[d, h], w[d], TN)
            return carry

        if first:
            acc[...] = jnp.zeros_like(acc)
        lax.fori_loop(0, 2 * n, body, 0)

    step(0, 1, whole)
    pass_on(0, 0)
    pass_on(0, 1)
    step(1, 1, whole)
    pass_on(0, 2)
    pass_on(0, 3)
    step(0, 2, whole)
    for i in range(2):
        ex_x_in(0, i).wait_recv()
    accumulate(pre, xt, wi, (0,), True)
    accumulate(pre, xt, wi, (1, 7))
    pass_on(1, 0)
    pass_on(1, 1)
    step(1, 2, [[(A, 0), (B, 1)], [(B, 0), (A, 1)]])
    for i in range(2, 4):
        ex_x_in(0, i).wait_recv()
    accumulate(pre, xt, wi, (2, 6))
    pass_on(1, 2)
    pass_on(1, 3)
    step(0, 3, [[(A, 0)], [(B, 0)]])
    accumulate(pre, xt, wi, (3, 5))
    for i in range(4):
        ex_x_in(1, i).wait_recv()
    accumulate(ga, dyt, wo, (0,), True)
    accumulate(ga, dyt, wo, (1, 7))
    accumulate(ga, dyt, wo, (2, 6))
    ag(1, 0, 3, A, 0).wait_recv()
    ag(1, 0, 4, A, 0).start()
    ag(1, 1, 3, B, 0).wait_recv()
    ag(1, 1, 4, B, 0).start()
    ag(0, 0, 4, A, 0).wait_recv()
    ag(0, 1, 4, B, 0).wait_recv()
    accumulate(pre, xt, wi, (4,))
    pre_cp = rc(pre, pre_in, core_s.at[0], core_r.at[0], other_core)
    pre_cp.start()
    bias_cp.wait_recv()
    bias = jnp.where(same, bias_in[0], bias_in[1])[0:1]
    pre_cp.wait_recv()

    def gelu(i, carry):
        h, rows = lax.div(i, 8), pl.ds(pl.multiple_of(lax.rem(i, 8) * 32, 32), 32)
        v = pre[h, rows] + pre_in[h, rows] + bias
        cdf = 0.5 * (1.0 + lax.erf(v * ROOT_HALF))
        act[h, rows] = (v * cdf).astype(BF16)
        slope[h, rows] = cdf + v * jnp.exp(-0.5 * v * v) * INV_ROOT_TWO_PI
        return carry

    lax.fori_loop(0, 16, gelu, 0)

    terms, rins, lins, ends = (term_o, term_i), (rin_o, rin_i), (lin_o, lin_i), (parts_o, parts_i)

    def make_terms(w, lo, hi):
        src, val, out = (dyt, xt)[w], (act, gp)[w], terms[w]

        def body(i, carry):
            d = lax.rem(4 + lax.div(i + 1, 2) * (2 * lax.rem(i, 2) - 1) + NZ, NZ)
            total = dot(src[d, 0], val[0], NN) + dot(src[d, 1], val[1], NN)
            out[d] = (total * scale).astype(BF16)
            return carry

        lax.fori_loop(lo, hi, body, 0)

    def rs(w, g, e, rows, part):
        buf = terms[w]
        d = NZ - e if g == 0 else e
        to = (right, left)[g] if e > 1 else (swap_r, swap_l)[g]
        dst = (rins, lins)[g][w].at[e - 2] if e > 1 else ends[w].at[1 + g]
        i = ((w * 2 + g) * 4 + e - 1) * 2 + part
        return rc(buf.at[d, rows], dst.at[rows], rs_s.at[i], rs_r.at[i], to)

    def add_in(w, g, e, rows):
        d = NZ - e if g == 0 else e
        came = (rins, lins)[g][w]
        buf = terms[w]
        buf[d, rows] = (buf[d, rows].astype(F32) + came[e - 1, rows].astype(F32)).astype(BF16)

    def hop(w, g, e, rows, part, rows_in=None, part_in=None):
        rs(w, g, e + 1, rows, part if part_in is None else part_in).wait_recv()
        add_in(w, g, e, rows)
        rs(w, g, e, rows, part).start()

    firsts = (A, B)
    seconds = (B, A)

    def own_copy(w):
        i = w
        return rc(terms[w].at[0], ends[w].at[0], own_s.at[i], own_r.at[i], swap)

    def own_local(w):
        return pltpu.make_async_copy(terms[w].at[0], ends[w].at[0], own_s.at[2 + w])

    def send_own(w):
        @pl.when(same)
        def _():
            own_local(w).start()

        @pl.when(jnp.logical_not(same))
        def _():
            own_copy(w).start()

    def wait_own(w):
        @pl.when(same)
        def _():
            own_local(w).wait()

        @pl.when(jnp.logical_not(same))
        def _():
            own_copy(w).wait()

    make_terms(0, 0, 3)
    for g in range(2):
        rs(0, g, 4, firsts[g], 0).start()
    for g in range(2):
        rs(0, g, 3, seconds[g], 1).start()
    ag(1, 0, 3, B, 1).wait_recv()
    ag(1, 1, 3, A, 1).wait_recv()
    accumulate(ga, dyt, wo, (3, 5))
    ag(1, 0, 4, A, 0).wait_recv()
    ag(1, 1, 4, B, 0).wait_recv()
    accumulate(ga, dyt, wo, (4,))
    ga_cp = rc(ga, ga_in, core_s.at[1], core_r.at[1], other_core)
    ga_cp.start()
    for g in range(2):
        hop(0, g, 3, firsts[g], 0)
    make_terms(0, 3, 8)
    send_own(0)
    ga_cp.wait_recv()

    def grad(i, carry):
        h, rows = lax.div(i, 8), pl.ds(pl.multiple_of(lax.rem(i, 8) * 32, 32), 32)
        gp[h, rows] = ((ga[h, rows] + ga_in[h, rows]) * slope[h, rows]).astype(BF16)
        return carry

    lax.fori_loop(0, 16, grad, 0)
    make_terms(1, 0, 3)
    for g in range(2):
        rs(1, g, 4, firsts[g], 0).start()
    for g in range(2):
        rs(1, g, 3, seconds[g], 1).start()
    make_terms(1, 3, 8)
    send_own(1)

    def dx_body(i, carry):
        k, h = lax.div(i, 2), lax.rem(i, 2)
        d = lax.rem(z + NZ - k, NZ)
        dxs[lax.div(k, 2), 2 * lax.rem(k, 2) + h] = dot(wi[d], gp[h], NT_DIMS).astype(BF16)
        return carry

    lax.fori_loop(0, 16, dx_body, 0)

    def x_sum(r):
        return rc(dxs.at[x_peer(r)], x_in.at[r - 1], dx_s.at[r - 1], dx_r.at[r - 1], x_dev(r))

    def y_sum(r):
        yl, ah = y_peer(r)
        return rc(ys.at[2 * yl + ah], y_in.at[r - 1], dx_s.at[r + 2], dx_r.at[r + 2], y_dev(r))

    for r in (1, 2, 3):
        x_sum(r).start()

    def both_halves(w, e):
        for g in range(2):
            rs(w, g, e + 1, seconds[g], 1).wait_recv()
            rs(w, g, e + 1, firsts[g], 0).wait_recv()
            add_in(w, g, e, FULL)
            rs(w, g, e, FULL, 0).start()

    both_halves(0, 2)
    for g in range(2):
        hop(1, g, 3, firsts[g], 0)
    for g in range(2):
        rs(0, g, 2, FULL, 0).wait_recv()
        add_in(0, g, 1, FULL)
        rs(0, g, 1, FULL, 0).start()
    for part, pick in ((1, seconds), (0, firsts)):
        for g in range(2):
            hop(1, g, 2, pick[g], part)

    for r in (1, 2, 3):
        x_sum(r).wait_recv()

    def x_body(i, carry):
        total = dxs[x_, i].astype(F32)
        for r in range(3):
            total = total + x_in[r, i].astype(F32)
        ys[i] = total.astype(BF16)
        return carry

    lax.fori_loop(0, 4, x_body, 0)
    for r in (1, 2, 3):
        y_sum(r).start()

    for part, pick in ((1, seconds), (0, firsts)):
        for g in range(2):
            hop(1, g, 1, pick[g], part)

    for r in (1, 2, 3):
        y_sum(r).wait_recv()
    total = ys[2 * ypar + a].astype(F32)
    for r in range(3):
        total = total + y_in[r].astype(F32)
    dx_v[...] = total.astype(BF16)
    put_dx.start()

    wait_own(0)
    for g in range(2):
        rs(0, g, 1, FULL, 0).wait_recv()

    wait_own(1)
    for part, pick in ((1, seconds), (0, firsts)):
        for g in range(2):
            rs(1, g, 1, pick[g], part).wait_recv()

    @pl.when(jnp.logical_not(same))
    def _():
        swap_wi.wait_send()
        swap_wo.wait_send()

    for w in range(2):
        for g in range(2):
            ag(w, g, 1, FULL, 0).wait_send()
            ag(w, g, 2, FULL, 0).wait_send()
            ag(w, g, 4, firsts[g], 0).wait_send()
        for i in range(4):
            ex_y(w, i).wait_send()
            ex_x(w, i).wait_send()
    for g in range(2):
        ag(0, g, 3, FULL, 0).wait_send()
        ag(1, g, 3, firsts[g], 0).wait_send()
        ag(1, g, 3, seconds[g], 1).wait_send()
    bias_cp.wait_send()
    pre_cp.wait_send()
    ga_cp.wait_send()
    for w in range(2):
        for g in range(2):
            rs(w, g, 4, firsts[g], 0).wait_send()
            rs(w, g, 3, seconds[g], 1).wait_send()
            rs(w, g, 3, firsts[g], 0).wait_send()
    for g in range(2):
        rs(0, g, 2, FULL, 0).wait_send()
        rs(0, g, 1, FULL, 0).wait_send()
        for e in (2, 1):
            rs(1, g, e, seconds[g], 1).wait_send()
            rs(1, g, e, firsts[g], 0).wait_send()
    for r in (1, 2, 3):
        x_sum(r).wait_send()
        y_sum(r).wait_send()
    put_dx.wait()


def finish(dx_ref, in_ref, out_ref, dx_out, dwin_out, dwout_out):
    dx_out[...] = dx_ref[...]
    for ref, out in ((in_ref, dwin_out), (out_ref, dwout_out)):
        out[...] = ref[0].astype(F32) + ref[1].astype(F32) + ref[2].astype(F32)


def per_device(inputs, upstream, w_in, bias_in, w_out):
    rows, width = inputs.shape
    scale = 1.0 / math.sqrt(rows * lax.axis_size("dp"))
    any_space = pl.BlockSpec(memory_space=pl.ANY)
    vmem = pl.BlockSpec(memory_space=pltpu.VMEM)
    shard = (SH, FC)
    ring = (NZ,) + shard
    acc = (2, ROWS, FC)
    turned = (NZ, 2, SH, ROWS)
    dx, parts_i, parts_o = pl.pallas_call(
        lambda *refs: kernel(scale, *refs),
        out_shape=(
            jax.ShapeDtypeStruct((SH, ROWS), BF16),
            jax.ShapeDtypeStruct((3,) + shard, BF16),
            jax.ShapeDtypeStruct((3,) + shard, BF16),
        ),
        in_specs=[any_space, any_space, any_space, any_space, vmem],
        out_specs=(any_space, any_space, any_space),
        scratch_shapes=[
            pltpu.VMEM((SH, ROWS), BF16),
            pltpu.VMEM((rows, width), BF16),
            pltpu.VMEM((rows, width), BF16),
            pltpu.VMEM(turned, BF16),
            pltpu.VMEM(turned, BF16),
            pltpu.VMEM(ring, BF16),
            pltpu.VMEM(ring, BF16),
            pltpu.VMEM(acc, F32),
            pltpu.VMEM(acc, F32),
            pltpu.VMEM(acc, BF16),
            pltpu.VMEM(acc, F32),
            pltpu.VMEM(acc, F32),
            pltpu.VMEM(acc, BF16),
            pltpu.VMEM(acc, F32),
            pltpu.VMEM(ring, BF16),
            pltpu.VMEM(ring, BF16),
            pltpu.VMEM((3,) + shard, BF16),
            pltpu.VMEM((3,) + shard, BF16),
            pltpu.VMEM((3,) + shard, BF16),
            pltpu.VMEM((3,) + shard, BF16),
            pltpu.VMEM((4, 4, SH, ROWS), BF16),
            pltpu.VMEM((3, 4, SH, ROWS), BF16),
            pltpu.VMEM((4, SH, ROWS), BF16),
            pltpu.VMEM((3, SH, ROWS), BF16),
            pltpu.VMEM((2, 8, FC), F32),
            pltpu.SemaphoreType.DMA((5,)),
            pltpu.SemaphoreType.DMA((2,)),
            pltpu.SemaphoreType.DMA((2,)),
            pltpu.SemaphoreType.DMA((32,)),
            pltpu.SemaphoreType.DMA((32,)),
            pltpu.SemaphoreType.DMA((16,)),
            pltpu.SemaphoreType.DMA((16,)),
            pltpu.SemaphoreType.DMA((3,)),
            pltpu.SemaphoreType.DMA((3,)),
            pltpu.SemaphoreType.DMA((32,)),
            pltpu.SemaphoreType.DMA((32,)),
            pltpu.SemaphoreType.DMA((4,)),
            pltpu.SemaphoreType.DMA((4,)),
            pltpu.SemaphoreType.DMA((6,)),
            pltpu.SemaphoreType.DMA((6,)),
        ],
        compiler_params=pltpu.CompilerParams(
            collective_id=0, has_side_effects=True, vmem_limit_bytes=60 * 1024 * 1024
        ),
    )(inputs, upstream, w_in, w_out.T, bias_in)
    steps = 4
    part_spec = pl.BlockSpec((3, SH // steps, FC), lambda i: (0, i, 0))
    dx_spec = pl.BlockSpec((SH // steps, ROWS), lambda i: (i, 0))
    dw_spec = pl.BlockSpec((SH // steps, FC), lambda i: (i, 0))
    dx, dwin, dwout = pl.pallas_call(
        finish,
        grid=(steps,),
        out_shape=(
            jax.ShapeDtypeStruct((SH, ROWS), BF16),
            jax.ShapeDtypeStruct(shard, F32),
            jax.ShapeDtypeStruct(shard, F32),
        ),
        in_specs=[dx_spec, part_spec, part_spec],
        out_specs=(dx_spec, dw_spec, dw_spec),
    )(dx, parts_i, parts_o)
    return dx.T, dwin, dwout.T


def solution(mesh):
    placed = (P("dp", None), P("dp", None), P("dp", "tensor"), P("tensor"), P("tensor", "dp"))
    return jax.shard_map(
        per_device,
        mesh=mesh,
        in_specs=placed,
        out_specs=(P("dp", "tensor"), P("dp", "tensor"), P("tensor", "dp")),
        check_vma=False,
    )
```

```python
import math

import jax
import jax.numpy as jnp
from jax import lax
from jax.experimental import pallas as pl
from jax.experimental.pallas import tpu as pltpu
from jax.sharding import PartitionSpec as P

MESH = pl.DeviceIdType.MESH
ROOT_HALF = 0.7071067811865476
INV_ROOT_TWO_PI = 0.3989422804014327
BF16 = jnp.bfloat16
F32 = jnp.float32

NZ = 8
NT = 8
ROWS = 256
SH = 320
HF = SH // 2
FC = 640
PARTS = (pl.ds(0, HF), pl.ds(HF, HF))

TN = (((0,), (0,)), ((), ()))
NN = (((1,), (0,)), ((), ()))
NT_DIMS = (((1,), (1,)), ((), ()))


def dot(lhs, rhs, dims):
    return lax.dot_general(lhs, rhs, dims, preferred_element_type=F32)


def kernel(
    scale, x_hbm, dy_hbm, win_hbm, wout_hbm, bias_ref,
    dx_out, parts_i, parts_o,
    dx_v, xv, dyv, xt, dyt, wi, wo,
    pre, pre_in, act, ga, ga_in, gp, slope,
    term_o, term_i, rin_o, rin_i, lin_o, lin_i,
    dxa, dxb, sum_a, sum_b, in_a, in_b, last_a, last_b, turn_v, bias_in,
    ld_sem, sw_s, sw_r, ag_s, ag_r, ex_s, ex_r, core_s, core_r,
    rs_s, rs_r, own_s, own_r, dx_s, dx_r,
):
    dp = lax.axis_index("dp")
    tn = lax.axis_index("tensor")
    z, a = lax.div(dp, 2), lax.rem(dp, 2)
    t2, b = lax.div(tn, 2), lax.rem(tn, 2)
    x_, ypar = lax.div(t2, 2), lax.rem(t2, 2)
    y_ = 2 * a + ypar
    xpar = lax.rem(x_, 2)
    same = a == b
    differ = a != b
    zr, zl = lax.rem(z + 1, NZ), lax.rem(z + NZ - 1, NZ)

    def dev(z_, t_, a_, b_):
        return {"dp": 2 * z_ + a_, "tensor": 2 * t_ + b_}

    right, left = dev(zr, t2, a, b), dev(zl, t2, a, b)
    other_core = dev(z, t2, a, 1 - b)
    y_side = dev(z, t2 + 1 - 2 * ypar, 1 - a, b)
    x_side = dev(z, t2 + 2 - 4 * xpar, a, b)

    def x_peer(r):
        return lax.rem(x_ + r, 4)

    def y_peer(r):
        yy = lax.rem(y_ + r, 4)
        return lax.rem(yy, 2), lax.div(yy, 2)

    def x_dev(r):
        return dev(z, 2 * x_peer(r) + ypar, a, b)

    def y_dev(r):
        yl, ah = y_peer(r)
        return dev(z, 2 * x_ + yl, ah, b)

    def rc(src, dst, ss, rs, to):
        return pltpu.make_async_remote_copy(
            src_ref=src, dst_ref=dst, send_sem=ss, recv_sem=rs, device_id=to, device_id_type=MESH
        )

    def part_rows(p):
        if isinstance(p, int):
            return PARTS[p]
        return pl.ds(pl.multiple_of(p * HF, HF), HF)

    hbm = (win_hbm, wout_hbm)
    weights = (wi, wo)
    here = part_rows(b)

    def ld_w(w):
        return pltpu.make_async_copy(hbm[w].at[here], weights[w].at[0, part_rows(a)], ld_sem.at[2 + w])

    ld_x = pltpu.make_async_copy(x_hbm, xv, ld_sem.at[0])
    ld_dy = pltpu.make_async_copy(dy_hbm, dyv, ld_sem.at[1])
    put_dx = pltpu.make_async_copy(dx_v, dx_out, ld_sem.at[4])

    @pl.when(same)
    def _():
        ld_w(0).start()
        ld_w(1).start()

    ld_x.start()
    ld_dy.start()

    barrier = pltpu.get_barrier_semaphore()

    def greet(to):
        pl.semaphore_signal(barrier, inc=1, device_id=to, device_id_type=MESH)

    for z_ in (zr, zl):
        for i in range(4):
            greet(dev(z_, t2, i // 2, i % 2))
    greet(other_core)
    greet(dev(z, t2, 1 - a, b))
    greet(dev(z, t2, 1 - a, 1 - b))
    for r in (1, 2, 3):
        greet(x_dev(r))
    greet(y_dev(1))
    greet(y_dev(3))
    pl.semaphore_wait(barrier, 16)

    def to_twin(w):
        rows = part_rows(a)
        return rc(hbm[w].at[part_rows(1 - b)], weights[w].at[0, rows], sw_s.at[2 * w], sw_r.at[2 * w], other_core)

    def to_chip(w, h):
        rows = part_rows(a)
        return rc(
            hbm[w].at[part_rows(h)], weights[w].at[0, rows], sw_s.at[2 * w + h], sw_r.at[2 * w + 1], dev(z, t2, b, h)
        )

    def from_twin(w):
        return rc(hbm[w].at[here], weights[w].at[0, part_rows(a)], sw_s.at[2 * w], sw_r.at[2 * w], other_core)

    def from_chip(w):
        return rc(hbm[w].at[here], weights[w].at[0, part_rows(1 - a)], sw_s.at[2 * w], sw_r.at[2 * w + 1], other_core)

    @pl.when(same)
    def _():
        to_twin(0).start()
        to_twin(1).start()

    @pl.when(differ)
    def _():
        for w in range(2):
            for h in range(2):
                to_chip(w, h).start()

    def ag(w, g, s, part):
        buf, rows = weights[w], part_rows(part)
        if g == 0:
            src, dst, to = s - 1, s, right
        else:
            src, dst, to = (NZ + 1 - s) % NZ, NZ - s, left
        i = ((w * 2 + g) * 4 + s - 1) * 2 + part
        return rc(buf.at[src, rows], buf.at[dst, rows], ag_s.at[i], ag_r.at[i], to)

    def send_first(w, part):
        for g in range(2):
            ag(w, g, 1, part).start()

    for w in range(2):
        @pl.when(same)
        def _():
            ld_w(w).wait()

        @pl.when(differ)
        def _():
            from_twin(w).wait_recv()

        send_first(w, a)

    bias_in[0] = jnp.broadcast_to(bias_ref[...].astype(F32)[None, :], (8, FC))
    bias_cp = rc(bias_in.at[0], bias_in.at[1], core_s.at[2], core_r.at[2], other_core)
    bias_cp.start()

    pairs = ((0, 1), (7, 2), (6, 3), (5, 4))

    def mine(i):
        p, q = pairs[i]
        return p + (q - p) * xpar

    def theirs(i):
        p, q = pairs[i]
        return q + (p - q) * xpar

    def turn(src, dst, d):
        k = lax.rem(z + NZ - d, NZ)
        v = src[:, pl.ds(pl.multiple_of(k * 2 * SH, 128), 2 * SH)].T
        first = b == 0
        dst[d, a, PARTS[0]] = jnp.where(first, v[:HF], v[HF:SH])
        dst[d, a, PARTS[1]] = jnp.where(first, v[SH : SH + HF], v[SH + HF :])

    rows_t = (xt, dyt)

    def ex_y(w, i):
        buf, d, m = rows_t[w], mine(i), w * 8 + i
        return rc(buf.at[d, a], buf.at[d, a], ex_s.at[m], ex_r.at[m], y_side)

    def ex_y_in(w, i):
        buf, d, m = rows_t[w], mine(i), w * 8 + i
        return rc(buf.at[d, 1 - a], buf.at[d, 1 - a], ex_s.at[m], ex_r.at[m], y_side)

    def ex_x(w, i):
        buf, d, m = rows_t[w], mine(i), w * 8 + 4 + i
        return rc(buf.at[d, 1 - a], buf.at[d, 1 - a], ex_s.at[m], ex_r.at[m], x_side)

    def ex_x_in(w, i):
        buf, d, m = rows_t[w], theirs(i), w * 8 + 4 + i
        return rc(buf.at[d, 1 - a], buf.at[d, 1 - a], ex_s.at[m], ex_r.at[m], x_side)

    ld_x.wait()
    for d in range(NZ):
        turn(xv, xt, d)

    for w in range(2):
        from_chip(w).wait_recv()
        send_first(w, 1 - a)

    for i in range(4):
        ex_y(0, i).start()
    ld_dy.wait()
    for d in range(NZ):
        turn(dyv, dyt, d)
    for i in range(4):
        ex_y(1, i).start()

    def pass_on(w, i):
        ex_y_in(w, i).wait_recv()
        ex_x(w, i).start()

    def step(w, s, part):
        for g in range(2):
            ag(w, g, s, part).wait_recv()
            ag(w, g, s + 1, part).start()

    def accumulate(acc, src, w, slots, first=False):
        n = len(slots)

        def body(i, carry):
            j, h = lax.div(i, 2), lax.rem(i, 2)
            d = slots[0] if n == 1 else slots[0] + j * (slots[1] - slots[0])
            acc[h] += dot(src[d, h], w[d], TN)
            return carry

        if first:
            acc[...] = jnp.zeros_like(acc)
        lax.fori_loop(0, 2 * n, body, 0)

    firsts = (0, 1)
    seconds = (1, 0)

    for w in range(2):
        step(w, 1, a)
        step(w, 1, 1 - a)
    for i in range(2):
        pass_on(0, i)
    step(0, 2, a)
    for i in range(2, 4):
        pass_on(0, i)
    step(0, 2, 1 - a)
    for i in range(2):
        ex_x_in(0, i).wait_recv()
    accumulate(pre, xt, wi, (0,), True)
    accumulate(pre, xt, wi, (1, 7))
    pass_on(1, 0)
    for i in range(2, 4):
        ex_x_in(0, i).wait_recv()
    accumulate(pre, xt, wi, (2, 6))
    pass_on(1, 1)
    for part in (a, 1 - a):
        for g in range(2):
            ag(1, g, 2, part).wait_recv()
    pass_on(1, 2)
    for g in range(2):
        ag(0, g, 3, firsts[g]).wait_recv()
        ag(0, g, 4, firsts[g]).start()
    for pick in (firsts, seconds):
        for g in range(2):
            ag(1, g, 3, pick[g]).start()
    pass_on(1, 3)
    for g in range(2):
        ag(0, g, 3, seconds[g]).wait_recv()
    accumulate(pre, xt, wi, (3, 5))
    for g in range(2):
        ag(0, g, 4, firsts[g]).wait_recv()
    accumulate(pre, xt, wi, (4,))
    pre_cp = rc(pre, pre_in, core_s.at[0], core_r.at[0], other_core)
    pre_cp.start()
    for i in range(4):
        ex_x_in(1, i).wait_recv()
    accumulate(ga, dyt, wo, (0,), True)
    accumulate(ga, dyt, wo, (1, 7))
    for g in range(2):
        ag(1, g, 3, firsts[g]).wait_recv()
        ag(1, g, 4, firsts[g]).start()
    accumulate(ga, dyt, wo, (2, 6))
    bias_cp.wait_recv()
    bias = jnp.where(same, bias_in[0], bias_in[1])[0:1]
    pre_cp.wait_recv()

    def gelu(i, carry):
        h, rows = lax.div(i, 8), pl.ds(pl.multiple_of(lax.rem(i, 8) * 32, 32), 32)
        v = pre[h, rows] + pre_in[h, rows] + bias
        cdf = 0.5 * (1.0 + lax.erf(v * ROOT_HALF))
        act[h, rows] = (v * cdf).astype(BF16)
        slope[h, rows] = cdf + v * jnp.exp(-0.5 * v * v) * INV_ROOT_TWO_PI
        return carry

    lax.fori_loop(0, 16, gelu, 0)

    terms, rins, lins, ends = (term_o, term_i), (rin_o, rin_i), (lin_o, lin_i), (parts_o, parts_i)

    def make_terms(w, lo, hi):
        src, val, out = (dyt, xt)[w], (act, gp)[w], terms[w]

        def body(i, carry):
            d = lax.rem(4 + lax.div(i + 1, 2) * (2 * lax.rem(i, 2) - 1) + NZ, NZ)
            total = dot(src[d, 0], val[0], NN) + dot(src[d, 1], val[1], NN)
            out[d] = (total * scale).astype(BF16)
            return carry

        lax.fori_loop(lo, hi, body, 0)

    def rs(w, g, e, part):
        rows = part_rows(part)
        src = terms[w].at[NZ - e if g == 0 else e, rows]
        i = (w * 2 + g) * 4 + e - 1
        if e > 1:
            dst, to, m = (rins, lins)[g][w].at[e - 2, rows], (right, left)[g], 2 * i + part
        else:
            dst, to, m = ends[w].at[1 + g, here], dev((zr, zl)[g], t2, part, a), 2 * i + b
        return rc(src, dst, rs_s.at[2 * i + part], rs_r.at[m], to)

    def rs_end(w, g, h):
        rows, m = PARTS[h], 2 * ((w * 2 + g) * 4) + h
        return rc(terms[w].at[0, rows], ends[w].at[1 + g, rows], rs_s.at[m], rs_r.at[m], right)

    def hop(w, g, e, part):
        rs(w, g, e + 1, part).wait_recv()
        d, rows = NZ - e if g == 0 else e, part_rows(part)
        buf, came = terms[w], (rins, lins)[g][w]
        buf[d, rows] = (buf[d, rows].astype(F32) + came[e - 1, rows].astype(F32)).astype(BF16)
        rs(w, g, e, part).start()

    def own_copy(w, p):
        return rc(
            terms[w].at[0, PARTS[p]], ends[w].at[0, here], own_s.at[2 * w + p], own_r.at[2 * w + b], dev(z, t2, p, a)
        )

    def own_local(w, p):
        return pltpu.make_async_copy(terms[w].at[0, PARTS[p]], ends[w].at[0, here], own_s.at[2 * w + p])

    def own_end(w, h):
        return rc(terms[w].at[0, PARTS[h]], ends[w].at[0, PARTS[h]], own_s.at[0], own_r.at[2 * w + h], right)

    def send_own(w):
        for p in range(2):
            stays = same & (a == p)

            @pl.when(stays)
            def _():
                own_local(w, p).start()

            @pl.when(jnp.logical_not(stays))
            def _():
                own_copy(w, p).start()

    def wait_own(w):
        for p in range(2):
            stays = same & (a == p)

            @pl.when(stays)
            def _():
                own_local(w, p).wait()

            @pl.when(jnp.logical_not(stays))
            def _():
                own_copy(w, p).wait_send()

        for h in range(2):
            @pl.when(jnp.logical_not(same & (b == h)))
            def _():
                own_end(w, h).wait_recv()

    make_terms(0, 0, 3)
    for g in range(2):
        rs(0, g, 4, firsts[g]).start()
    for g in range(2):
        rs(0, g, 3, seconds[g]).start()
    for g in range(2):
        ag(1, g, 3, seconds[g]).wait_recv()
    accumulate(ga, dyt, wo, (3, 5))
    for g in range(2):
        ag(1, g, 4, firsts[g]).wait_recv()
    accumulate(ga, dyt, wo, (4,))
    ga_cp = rc(ga, ga_in, core_s.at[1], core_r.at[1], other_core)
    ga_cp.start()
    make_terms(0, 3, 8)
    for g in range(2):
        hop(0, g, 3, firsts[g])
    send_own(0)
    ga_cp.wait_recv()

    def grad(i, carry):
        h, rows = lax.div(i, 8), pl.ds(pl.multiple_of(lax.rem(i, 8) * 32, 32), 32)
        gp[h, rows] = ((ga[h, rows] + ga_in[h, rows]) * slope[h, rows]).astype(BF16)
        return carry

    lax.fori_loop(0, 16, grad, 0)
    make_terms(1, 0, 3)
    for g in range(2):
        rs(1, g, 4, firsts[g]).start()
    for g in range(2):
        rs(1, g, 3, seconds[g]).start()

    def dx_body(i, carry):
        k, h = lax.div(i, 2), lax.rem(i, 2)
        d = lax.rem(z + NZ - k, NZ)
        v = dot(wi[d], gp[h], NT_DIMS).astype(BF16)
        xx, yy = lax.div(k, 2), 2 * lax.rem(k, 2) + h
        dxa[xx, yy] = v[:HF]
        dxb[yy, xx] = v[HF:]
        return carry

    lax.fori_loop(0, 16, dx_body, 0)
    yy_ = 2 * ypar + a

    def y_index(r):
        yl, ah = y_peer(r)
        return 2 * yl + ah

    def first_a(r):
        return rc(dxa.at[x_peer(r)], in_a.at[r - 1], dx_s.at[r - 1], dx_r.at[r - 1], x_dev(r))

    def first_b(r):
        return rc(dxb.at[y_index(r)], in_b.at[r - 1], dx_s.at[r + 2], dx_r.at[r + 2], y_dev(r))

    def second_a(r):
        return rc(sum_a.at[y_index(r)], last_a.at[r - 1], dx_s.at[r + 5], dx_r.at[r + 5], y_dev(r))

    def second_b(r):
        return rc(sum_b.at[x_peer(r)], last_b.at[r - 1], dx_s.at[r + 8], dx_r.at[r + 8], x_dev(r))

    for r in (1, 2, 3):
        first_a(r).start()
        first_b(r).start()

    make_terms(1, 3, 8)
    send_own(1)
    for pick in (seconds, firsts):
        for g in range(2):
            hop(0, g, 2, pick[g])
    for g in range(2):
        hop(1, g, 3, firsts[g])
    for pick in (seconds, firsts):
        for g in range(2):
            hop(0, g, 1, pick[g])

    for r in (1, 2, 3):
        first_a(r).wait_recv()
        first_b(r).wait_recv()

    def sum_body(i, carry):
        total_a, total_b = dxa[x_, i].astype(F32), dxb[yy_, i].astype(F32)
        for r in range(3):
            total_a = total_a + in_a[r, i].astype(F32)
            total_b = total_b + in_b[r, i].astype(F32)
        sum_a[i], sum_b[i] = total_a.astype(BF16), total_b.astype(BF16)
        return carry

    lax.fori_loop(0, 4, sum_body, 0)
    for r in (1, 2, 3):
        second_a(r).start()
        second_b(r).start()

    for pick in (seconds, firsts):
        for g in range(2):
            hop(1, g, 2, pick[g])

    for pick in (seconds, firsts):
        for g in range(2):
            hop(1, g, 1, pick[g])

    for r in (1, 2, 3):
        second_a(r).wait_recv()
        second_b(r).wait_recv()
    total_a, total_b = sum_a[yy_].astype(F32), sum_b[x_].astype(F32)
    for r in range(3):
        total_a = total_a + last_a[r].astype(F32)
        total_b = total_b + last_b[r].astype(F32)
    total_a, total_b = total_a.astype(BF16), total_b.astype(BF16)
    dx_v[here] = jnp.where(b == 0, total_a, total_b)
    turn_v[...] = jnp.where(b == 0, total_b, total_a)
    dx_cp = rc(turn_v, dx_v.at[here], core_s.at[3], core_r.at[3], other_core)
    dx_cp.start()

    rc(turn_v, dx_v.at[part_rows(1 - b)], core_s.at[3], core_r.at[3], other_core).wait_recv()
    put_dx.start()

    for w in range(2):
        wait_own(w)
        for g in range(2):
            for h in range(2):
                rs_end(w, g, h).wait_recv()

    @pl.when(same)
    def _():
        to_twin(0).wait_send()
        to_twin(1).wait_send()

    @pl.when(differ)
    def _():
        for w in range(2):
            for h in range(2):
                to_chip(w, h).wait_send()

    for w in range(2):
        for g in range(2):
            for s in (1, 2, 3):
                for part in range(2):
                    ag(w, g, s, part).wait_send()
            ag(w, g, 4, firsts[g]).wait_send()
        for i in range(4):
            ex_y(w, i).wait_send()
            ex_x(w, i).wait_send()
    for cp in (bias_cp, pre_cp, ga_cp, dx_cp):
        cp.wait_send()
    for w in range(2):
        for g in range(2):
            rs(w, g, 4, firsts[g]).wait_send()
            for e in (3, 2, 1):
                for part in range(2):
                    rs(w, g, e, part).wait_send()
    for r in (1, 2, 3):
        for cp in (first_a(r), first_b(r), second_a(r), second_b(r)):
            cp.wait_send()
    put_dx.wait()


def finish(dx_ref, in_ref, out_ref, dx_out, dwin_out, dwout_out):
    dx_out[...] = dx_ref[...]
    for ref, out in ((in_ref, dwin_out), (out_ref, dwout_out)):
        out[...] = ref[0].astype(F32) + ref[1].astype(F32) + ref[2].astype(F32)


def per_device(inputs, upstream, w_in, bias_in, w_out):
    rows, width = inputs.shape
    scale = 1.0 / math.sqrt(rows * lax.axis_size("dp"))
    any_space = pl.BlockSpec(memory_space=pl.ANY)
    vmem = pl.BlockSpec(memory_space=pltpu.VMEM)
    shard = (SH, FC)
    ring = (NZ,) + shard
    acc = (2, ROWS, FC)
    turned = (NZ, 2, SH, ROWS)
    dx, parts_i, parts_o = pl.pallas_call(
        lambda *refs: kernel(scale, *refs),
        out_shape=(
            jax.ShapeDtypeStruct((SH, ROWS), BF16),
            jax.ShapeDtypeStruct((3,) + shard, BF16),
            jax.ShapeDtypeStruct((3,) + shard, BF16),
        ),
        in_specs=[any_space, any_space, any_space, any_space, vmem],
        out_specs=(any_space, any_space, any_space),
        scratch_shapes=[
            pltpu.VMEM((SH, ROWS), BF16),
            pltpu.VMEM((rows, width), BF16),
            pltpu.VMEM((rows, width), BF16),
            pltpu.VMEM(turned, BF16),
            pltpu.VMEM(turned, BF16),
            pltpu.VMEM(ring, BF16),
            pltpu.VMEM(ring, BF16),
            pltpu.VMEM(acc, F32),
            pltpu.VMEM(acc, F32),
            pltpu.VMEM(acc, BF16),
            pltpu.VMEM(acc, F32),
            pltpu.VMEM(acc, F32),
            pltpu.VMEM(acc, BF16),
            pltpu.VMEM(acc, F32),
            pltpu.VMEM(ring, BF16),
            pltpu.VMEM(ring, BF16),
            pltpu.VMEM((3,) + shard, BF16),
            pltpu.VMEM((3,) + shard, BF16),
            pltpu.VMEM((3,) + shard, BF16),
            pltpu.VMEM((3,) + shard, BF16),
            pltpu.VMEM((4, 4, HF, ROWS), BF16),
            pltpu.VMEM((4, 4, HF, ROWS), BF16),
            pltpu.VMEM((4, HF, ROWS), BF16),
            pltpu.VMEM((4, HF, ROWS), BF16),
            pltpu.VMEM((3, 4, HF, ROWS), BF16),
            pltpu.VMEM((3, 4, HF, ROWS), BF16),
            pltpu.VMEM((3, HF, ROWS), BF16),
            pltpu.VMEM((3, HF, ROWS), BF16),
            pltpu.VMEM((HF, ROWS), BF16),
            pltpu.VMEM((2, 8, FC), F32),
            pltpu.SemaphoreType.DMA((5,)),
            pltpu.SemaphoreType.DMA((4,)),
            pltpu.SemaphoreType.DMA((4,)),
            pltpu.SemaphoreType.DMA((32,)),
            pltpu.SemaphoreType.DMA((32,)),
            pltpu.SemaphoreType.DMA((16,)),
            pltpu.SemaphoreType.DMA((16,)),
            pltpu.SemaphoreType.DMA((4,)),
            pltpu.SemaphoreType.DMA((4,)),
            pltpu.SemaphoreType.DMA((32,)),
            pltpu.SemaphoreType.DMA((32,)),
            pltpu.SemaphoreType.DMA((4,)),
            pltpu.SemaphoreType.DMA((4,)),
            pltpu.SemaphoreType.DMA((12,)),
            pltpu.SemaphoreType.DMA((12,)),
        ],
        compiler_params=pltpu.CompilerParams(
            collective_id=0, has_side_effects=True, vmem_limit_bytes=60 * 1024 * 1024
        ),
    )(inputs, upstream, w_in, w_out.T, bias_in)
    steps = 2
    part_spec = pl.BlockSpec((3, SH // steps, FC), lambda i: (0, i, 0))
    dx_spec = pl.BlockSpec((SH // steps, ROWS), lambda i: (i, 0))
    dw_spec = pl.BlockSpec((SH // steps, FC), lambda i: (i, 0))
    dx, dwin, dwout = pl.pallas_call(
        finish,
        grid=(steps,),
        out_shape=(
            jax.ShapeDtypeStruct((SH, ROWS), BF16),
            jax.ShapeDtypeStruct(shard, F32),
            jax.ShapeDtypeStruct(shard, F32),
        ),
        in_specs=[dx_spec, part_spec, part_spec],
        out_specs=(dx_spec, dw_spec, dw_spec),
    )(dx, parts_i, parts_o)
    return dx.T, dwin, dwout.T


def solution(mesh):
    placed = (P("dp", None), P("dp", None), P("dp", "tensor"), P("tensor"), P("tensor", "dp"))
    return jax.shard_map(
        per_device,
        mesh=mesh,
        in_specs=placed,
        out_specs=(P("dp", "tensor"), P("dp", "tensor"), P("tensor", "dp")),
        check_vma=False,
    )
```

```python
import math

import jax
import jax.numpy as jnp
from jax import lax
from jax.experimental import pallas as pl
from jax.experimental.pallas import tpu as pltpu
from jax.sharding import PartitionSpec as P

MESH = pl.DeviceIdType.MESH
ROOT_HALF = 0.7071067811865476
INV_ROOT_TWO_PI = 0.3989422804014327
BF16 = jnp.bfloat16
F32 = jnp.float32

NZ = 8
NT = 8
ROWS = 256
SH = 320
HF = SH // 2
FC = 640
PARTS = (pl.ds(0, HF), pl.ds(HF, HF))

TN = (((0,), (0,)), ((), ()))
NN = (((1,), (0,)), ((), ()))
NT_DIMS = (((1,), (1,)), ((), ()))


def dot(lhs, rhs, dims):
    return lax.dot_general(lhs, rhs, dims, preferred_element_type=F32)


def kernel(
    scale, x_hbm, dy_hbm, win_hbm, wout_hbm, bias_ref,
    dx_out, parts_i, parts_o,
    dx_v, xv, dyv, xt, dyt, wi, wo,
    pre, pre_in, act, ga, ga_in, gp, slope,
    term_o, term_i, rin_o, rin_i, lin_o, lin_i,
    dxa, dxb, sum_a, sum_b, in_a, in_b, last_a, last_b, turn_v, bias_in,
    ld_sem, sw_s, sw_r, ag_s, ag_r, ex_s, ex_r, core_s, core_r,
    rs_s, rs_r, own_s, own_r, dx_s, dx_r,
):
    dp = lax.axis_index("dp")
    tn = lax.axis_index("tensor")
    z, a = lax.div(dp, 2), lax.rem(dp, 2)
    t2, b = lax.div(tn, 2), lax.rem(tn, 2)
    x_, ypar = lax.div(t2, 2), lax.rem(t2, 2)
    y_ = 2 * a + ypar
    xpar = lax.rem(x_, 2)
    same = a == b
    differ = a != b
    zr, zl = lax.rem(z + 1, NZ), lax.rem(z + NZ - 1, NZ)

    def dev(z_, t_, a_, b_):
        return {"dp": 2 * z_ + a_, "tensor": 2 * t_ + b_}

    right, left = dev(zr, t2, a, b), dev(zl, t2, a, b)
    other_core = dev(z, t2, a, 1 - b)
    y_side = dev(z, t2 + 1 - 2 * ypar, 1 - a, b)
    x_side = dev(z, t2 + 2 - 4 * xpar, a, b)

    def x_peer(r):
        return lax.rem(x_ + r, 4)

    def y_peer(r):
        yy = lax.rem(y_ + r, 4)
        return lax.rem(yy, 2), lax.div(yy, 2)

    def x_dev(r):
        return dev(z, 2 * x_peer(r) + ypar, a, b)

    def y_dev(r):
        yl, ah = y_peer(r)
        return dev(z, 2 * x_ + yl, ah, b)

    def rc(src, dst, ss, rs, to):
        return pltpu.make_async_remote_copy(
            src_ref=src, dst_ref=dst, send_sem=ss, recv_sem=rs, device_id=to, device_id_type=MESH
        )

    def part_rows(p):
        if isinstance(p, int):
            return PARTS[p]
        return pl.ds(pl.multiple_of(p * HF, HF), HF)

    hbm = (win_hbm, wout_hbm)
    weights = (wi, wo)
    here = part_rows(b)

    def ld_w(w):
        return pltpu.make_async_copy(hbm[w].at[here], weights[w].at[0, part_rows(a)], ld_sem.at[2 + w])

    ld_x = pltpu.make_async_copy(x_hbm, xv, ld_sem.at[0])
    ld_dy = pltpu.make_async_copy(dy_hbm, dyv, ld_sem.at[1])
    put_dx = pltpu.make_async_copy(dx_v, dx_out, ld_sem.at[4])

    @pl.when(same)
    def _():
        ld_w(0).start()
        ld_w(1).start()

    ld_x.start()
    ld_dy.start()

    barrier = pltpu.get_barrier_semaphore()

    def greet(to):
        pl.semaphore_signal(barrier, inc=1, device_id=to, device_id_type=MESH)

    for z_ in (zr, zl):
        greet(dev(z_, t2, a, b))
        greet(dev(z_, t2, a, 1 - b))
    greet(other_core)
    greet(dev(z, t2, 1 - a, b))
    greet(dev(z, t2, 1 - a, 1 - b))
    for r in (1, 2, 3):
        greet(x_dev(r))
    greet(y_dev(1))
    greet(y_dev(3))
    pl.semaphore_wait(barrier, 12)

    def to_twin(w):
        rows = part_rows(a)
        return rc(hbm[w].at[part_rows(1 - b)], weights[w].at[0, rows], sw_s.at[2 * w], sw_r.at[2 * w], other_core)

    def to_chip(w, h):
        rows = part_rows(a)
        return rc(
            hbm[w].at[part_rows(h)], weights[w].at[0, rows], sw_s.at[2 * w + h], sw_r.at[2 * w + 1], dev(z, t2, b, h)
        )

    def from_twin(w):
        return rc(hbm[w].at[here], weights[w].at[0, part_rows(a)], sw_s.at[2 * w], sw_r.at[2 * w], other_core)

    def from_chip(w):
        return rc(hbm[w].at[here], weights[w].at[0, part_rows(1 - a)], sw_s.at[2 * w], sw_r.at[2 * w + 1], other_core)

    @pl.when(same)
    def _():
        to_twin(0).start()
        to_twin(1).start()

    @pl.when(differ)
    def _():
        for w in range(2):
            for h in range(2):
                to_chip(w, h).start()

    def ag(w, g, s, part):
        buf, rows = weights[w], part_rows(part)
        if g == 0:
            src, dst, to = s - 1, s, right
        else:
            src, dst, to = (NZ + 1 - s) % NZ, NZ - s, left
        i = ((w * 2 + g) * 4 + s - 1) * 2 + part
        return rc(buf.at[src, rows], buf.at[dst, rows], ag_s.at[i], ag_r.at[i], to)

    def send_first(w, part):
        for g in range(2):
            ag(w, g, 1, part).start()

    for w in range(2):
        @pl.when(same)
        def _():
            ld_w(w).wait()

        @pl.when(differ)
        def _():
            from_twin(w).wait_recv()

        send_first(w, a)

    bias_in[0] = jnp.broadcast_to(bias_ref[...].astype(F32)[None, :], (8, FC))
    bias_cp = rc(bias_in.at[0], bias_in.at[1], core_s.at[2], core_r.at[2], other_core)
    bias_cp.start()

    pairs = ((0, 1), (7, 2), (6, 3), (5, 4))

    def mine(i):
        p, q = pairs[i]
        return p + (q - p) * xpar

    def theirs(i):
        p, q = pairs[i]
        return q + (p - q) * xpar

    def turn(src, dst, d):
        k = lax.rem(z + NZ - d, NZ)
        v = src[:, pl.ds(pl.multiple_of(k * 2 * SH, 128), 2 * SH)].T
        first = b == 0
        dst[d, a, PARTS[0]] = jnp.where(first, v[:HF], v[HF:SH])
        dst[d, a, PARTS[1]] = jnp.where(first, v[SH : SH + HF], v[SH + HF :])

    rows_t = (xt, dyt)

    def ex_y(w, i):
        buf, d, m = rows_t[w], mine(i), w * 8 + i
        return rc(buf.at[d, a], buf.at[d, a], ex_s.at[m], ex_r.at[m], y_side)

    def ex_y_in(w, i):
        buf, d, m = rows_t[w], mine(i), w * 8 + i
        return rc(buf.at[d, 1 - a], buf.at[d, 1 - a], ex_s.at[m], ex_r.at[m], y_side)

    def ex_x(w, i):
        buf, d, m = rows_t[w], mine(i), w * 8 + 4 + i
        return rc(buf.at[d, 1 - a], buf.at[d, 1 - a], ex_s.at[m], ex_r.at[m], x_side)

    def ex_x_in(w, i):
        buf, d, m = rows_t[w], theirs(i), w * 8 + 4 + i
        return rc(buf.at[d, 1 - a], buf.at[d, 1 - a], ex_s.at[m], ex_r.at[m], x_side)

    ld_x.wait()
    for d in range(NZ):
        turn(xv, xt, d)

    for w in range(2):
        from_chip(w).wait_recv()
        send_first(w, 1 - a)

    for i in range(4):
        ex_y(0, i).start()
    ld_dy.wait()
    for d in range(NZ):
        turn(dyv, dyt, d)
    for i in range(4):
        ex_y(1, i).start()

    def pass_on(w, i):
        ex_y_in(w, i).wait_recv()
        ex_x(w, i).start()

    def step(w, s, part):
        for g in range(2):
            ag(w, g, s, part).wait_recv()
            ag(w, g, s + 1, part).start()

    def accumulate(acc, src, w, slots, first=False):
        n = len(slots)

        def body(i, carry):
            j, h = lax.div(i, 2), lax.rem(i, 2)
            d = slots[0] if n == 1 else slots[0] + j * (slots[1] - slots[0])
            acc[h] += dot(src[d, h], w[d], TN)
            return carry

        if first:
            acc[...] = jnp.zeros_like(acc)
        lax.fori_loop(0, 2 * n, body, 0)

    firsts = (0, 1)
    seconds = (1, 0)

    for w in range(2):
        step(w, 1, a)
        step(w, 1, 1 - a)
    for i in range(2):
        pass_on(0, i)
    for part in (a, 1 - a):
        for g in range(2):
            ag(0, g, 2, part).wait_recv()
    for pick in (firsts, seconds):
        for g in range(2):
            ag(0, g, 3, pick[g]).start()
    for i in range(2, 4):
        pass_on(0, i)
    for i in range(2):
        ex_x_in(0, i).wait_recv()
    accumulate(pre, xt, wi, (0,), True)
    accumulate(pre, xt, wi, (1, 7))
    pass_on(1, 0)
    for i in range(2, 4):
        ex_x_in(0, i).wait_recv()
    accumulate(pre, xt, wi, (2, 6))
    pass_on(1, 1)
    for part in (a, 1 - a):
        for g in range(2):
            ag(1, g, 2, part).wait_recv()
    pass_on(1, 2)
    for g in range(2):
        ag(0, g, 3, firsts[g]).wait_recv()
        ag(0, g, 4, firsts[g]).start()
    for pick in (firsts, seconds):
        for g in range(2):
            ag(1, g, 3, pick[g]).start()
    pass_on(1, 3)
    for g in range(2):
        ag(0, g, 3, seconds[g]).wait_recv()
    accumulate(pre, xt, wi, (3, 5))
    for g in range(2):
        ag(0, g, 4, firsts[g]).wait_recv()
    accumulate(pre, xt, wi, (4,))
    pre_cp = rc(pre, pre_in, core_s.at[0], core_r.at[0], other_core)
    pre_cp.start()
    for i in range(4):
        ex_x_in(1, i).wait_recv()
    accumulate(ga, dyt, wo, (0,), True)
    accumulate(ga, dyt, wo, (1, 7))
    for g in range(2):
        ag(1, g, 3, firsts[g]).wait_recv()
        ag(1, g, 4, firsts[g]).start()
    accumulate(ga, dyt, wo, (2, 6))
    bias_cp.wait_recv()
    bias = jnp.where(same, bias_in[0], bias_in[1])[0:1]
    pre_cp.wait_recv()

    def gelu(i, carry):
        h, rows = lax.div(i, 8), pl.ds(pl.multiple_of(lax.rem(i, 8) * 32, 32), 32)
        v = pre[h, rows] + pre_in[h, rows] + bias
        cdf = 0.5 * (1.0 + lax.erf(v * ROOT_HALF))
        act[h, rows] = (v * cdf).astype(BF16)
        slope[h, rows] = cdf + v * jnp.exp(-0.5 * v * v) * INV_ROOT_TWO_PI
        return carry

    lax.fori_loop(0, 16, gelu, 0)

    terms, rins, lins, ends = (term_o, term_i), (rin_o, rin_i), (lin_o, lin_i), (parts_o, parts_i)

    def make_terms(w, lo, hi):
        src, val, out = (dyt, xt)[w], (act, gp)[w], terms[w]

        def body(i, carry):
            d = lax.rem(4 + lax.div(i + 1, 2) * (2 * lax.rem(i, 2) - 1) + NZ, NZ)
            total = dot(src[d, 0], val[0], NN) + dot(src[d, 1], val[1], NN)
            out[d] = (total * scale).astype(BF16)
            return carry

        lax.fori_loop(lo, hi, body, 0)

    def rs(w, g, e, part, last=False):
        rows = part_rows(part)
        src = terms[w].at[NZ - e if g == 0 else e, rows]
        i = ((w * 2 + g) * 4 + e - 1) * 2 + part
        if last:
            m = 4 + (w * 2 + g) * 2 + b
            return rc(src, ends[w].at[1 + g, here], rs_s.at[i], own_r.at[m], dev((zr, zl)[g], t2, a, a))
        return rc(src, (rins, lins)[g][w].at[e - 1, rows], rs_s.at[i], rs_r.at[i], (right, left)[g])

    def last_in(w, g, h):
        m = 4 + (w * 2 + g) * 2 + h
        return rc(terms[w].at[0, PARTS[h]], ends[w].at[1 + g, PARTS[h]], own_s.at[0], own_r.at[m], right)

    def hop(w, g, e, part, last=False):
        rs(w, g, e + 1, part).wait_recv()
        d, rows = NZ - e if g == 0 else e, part_rows(part)
        buf, came = terms[w], (rins, lins)[g][w]
        buf[d, rows] = (buf[d, rows].astype(F32) + came[e, rows].astype(F32)).astype(BF16)
        rs(w, g, e, part, last).start()

    def end_copy(w, part):
        m = 2 * w + part
        return rc(
            terms[w].at[0, part_rows(part)], ends[w].at[0, here], own_s.at[m], own_r.at[2 * w + b], dev(z, t2, part, a)
        )

    def end_local(w):
        return pltpu.make_async_copy(terms[w].at[0, part_rows(a)], ends[w].at[0, here], own_s.at[2 * w + a])

    def end_in(w, h):
        return rc(terms[w].at[0, PARTS[h]], ends[w].at[0, PARTS[h]], own_s.at[0], own_r.at[2 * w + h], right)

    def send_own(w):
        @pl.when(same)
        def _():
            end_local(w).start()

        @pl.when(differ)
        def _():
            end_copy(w, a).start()

    def send_sum(w):
        rows = part_rows(1 - a)
        for g in range(2):
            rs(w, g, 1, 1 - a).wait_recv()
        total = terms[w][0, rows].astype(F32)
        for came in (rins[w], lins[w]):
            total = total + came[0, rows].astype(F32)
        terms[w][0, rows] = total.astype(BF16)
        end_copy(w, 1 - a).start()

    def wait_end(w):
        @pl.when(same)
        def _():
            end_local(w).wait()
            for g in range(2):
                for h in range(2):
                    last_in(w, g, h).wait_recv()

        @pl.when(differ)
        def _():
            end_copy(w, a).wait_send()

        end_copy(w, 1 - a).wait_send()
        for h in range(2):
            @pl.when(jnp.logical_not(same & (b == h)))
            def _():
                end_in(w, h).wait_recv()

    make_terms(0, 0, 3)
    for g in range(2):
        rs(0, g, 4, firsts[g]).start()
    for g in range(2):
        rs(0, g, 3, seconds[g]).start()
    for g in range(2):
        ag(1, g, 3, seconds[g]).wait_recv()
    accumulate(ga, dyt, wo, (3, 5))
    for g in range(2):
        ag(1, g, 4, firsts[g]).wait_recv()
    accumulate(ga, dyt, wo, (4,))
    ga_cp = rc(ga, ga_in, core_s.at[1], core_r.at[1], other_core)
    ga_cp.start()
    make_terms(0, 3, 8)
    for g in range(2):
        hop(0, g, 3, firsts[g])
    send_own(0)
    ga_cp.wait_recv()

    def grad(i, carry):
        h, rows = lax.div(i, 8), pl.ds(pl.multiple_of(lax.rem(i, 8) * 32, 32), 32)
        gp[h, rows] = ((ga[h, rows] + ga_in[h, rows]) * slope[h, rows]).astype(BF16)
        return carry

    lax.fori_loop(0, 16, grad, 0)
    make_terms(1, 0, 3)
    for g in range(2):
        rs(1, g, 4, firsts[g]).start()
    for g in range(2):
        rs(1, g, 3, seconds[g]).start()

    def dx_body(i, carry):
        k, h = lax.div(i, 2), lax.rem(i, 2)
        d = lax.rem(z + NZ - k, NZ)
        v = dot(wi[d], gp[h], NT_DIMS).astype(BF16)
        xx, yy = lax.div(k, 2), 2 * lax.rem(k, 2) + h
        dxa[xx, yy] = v[:HF]
        dxb[yy, xx] = v[HF:]
        return carry

    lax.fori_loop(0, 16, dx_body, 0)
    yy_ = 2 * ypar + a

    def y_index(r):
        yl, ah = y_peer(r)
        return 2 * yl + ah

    def first_a(r):
        return rc(dxa.at[x_peer(r)], in_a.at[r - 1], dx_s.at[r - 1], dx_r.at[r - 1], x_dev(r))

    def first_b(r):
        return rc(dxb.at[y_index(r)], in_b.at[r - 1], dx_s.at[r + 2], dx_r.at[r + 2], y_dev(r))

    def second_a(r):
        return rc(sum_a.at[y_index(r)], last_a.at[r - 1], dx_s.at[r + 5], dx_r.at[r + 5], y_dev(r))

    def second_b(r):
        return rc(sum_b.at[x_peer(r)], last_b.at[r - 1], dx_s.at[r + 8], dx_r.at[r + 8], x_dev(r))

    for r in (1, 2, 3):
        first_a(r).start()
        first_b(r).start()

    make_terms(1, 3, 8)
    send_own(1)
    for part in (1 - a, a):
        for g in range(2):
            hop(0, g, 2, part)
    for g in range(2):
        hop(1, g, 3, firsts[g])
    for g in range(2):
        hop(1, g, 2, 1 - a)
    for g in range(2):
        hop(0, g, 1, 1 - a)
    for g in range(2):
        hop(1, g, 2, a)

    for r in (1, 2, 3):
        first_a(r).wait_recv()
        first_b(r).wait_recv()

    def sum_body(i, carry):
        total_a, total_b = dxa[x_, i].astype(F32), dxb[yy_, i].astype(F32)
        for r in range(3):
            total_a = total_a + in_a[r, i].astype(F32)
            total_b = total_b + in_b[r, i].astype(F32)
        sum_a[i], sum_b[i] = total_a.astype(BF16), total_b.astype(BF16)
        return carry

    lax.fori_loop(0, 4, sum_body, 0)
    for r in (1, 2, 3):
        second_a(r).start()
        second_b(r).start()

    for g in range(2):
        hop(1, g, 1, 1 - a)
    for g in range(2):
        hop(0, g, 1, a, True)
    send_sum(0)
    for g in range(2):
        hop(1, g, 1, a, True)
    send_sum(1)

    for r in (1, 2, 3):
        second_a(r).wait_recv()
        second_b(r).wait_recv()
    total_a, total_b = sum_a[yy_].astype(F32), sum_b[x_].astype(F32)
    for r in range(3):
        total_a = total_a + last_a[r].astype(F32)
        total_b = total_b + last_b[r].astype(F32)
    total_a, total_b = total_a.astype(BF16), total_b.astype(BF16)
    dx_v[here] = jnp.where(b == 0, total_a, total_b)
    turn_v[...] = jnp.where(b == 0, total_b, total_a)
    dx_cp = rc(turn_v, dx_v.at[here], core_s.at[3], core_r.at[3], other_core)
    dx_cp.start()

    rc(turn_v, dx_v.at[part_rows(1 - b)], core_s.at[3], core_r.at[3], other_core).wait_recv()
    put_dx.start()


    @pl.when(same)
    def _():
        to_twin(0).wait_send()
        to_twin(1).wait_send()

    @pl.when(differ)
    def _():
        for w in range(2):
            for h in range(2):
                to_chip(w, h).wait_send()

    for w in range(2):
        for g in range(2):
            for s in (1, 2, 3):
                for part in range(2):
                    ag(w, g, s, part).wait_send()
            ag(w, g, 4, firsts[g]).wait_send()
        for i in range(4):
            ex_y(w, i).wait_send()
            ex_x(w, i).wait_send()
    for cp in (bias_cp, pre_cp, ga_cp):
        cp.wait_send()
    for w in range(2):
        for g in range(2):
            rs(w, g, 4, firsts[g]).wait_send()
            for e in (3, 2) if w else (3, 2, 1):
                for part in range(2):
                    rs(w, g, e, part).wait_send()
    for r in (1, 2, 3):
        for cp in (first_a(r), first_b(r), second_a(r), second_b(r)):
            cp.wait_send()

    wait_end(0)
    wait_end(1)
    for g in range(2):
        for part in range(2):
            rs(1, g, 1, part).wait_send()
    dx_cp.wait_send()
    put_dx.wait()


def finish(dx_ref, in_ref, out_ref, dx_out, dwin_out, dwout_out):
    dx_out[...] = dx_ref[...]
    whole = lax.rem(lax.axis_index("dp"), 2) != lax.rem(lax.axis_index("tensor"), 2)
    for ref, out in ((in_ref, dwin_out), (out_ref, dwout_out)):
        @pl.when(whole)
        def _():
            out[...] = ref[0].astype(F32)

        @pl.when(jnp.logical_not(whole))
        def _():
            out[...] = ref[0].astype(F32) + ref[1].astype(F32) + ref[2].astype(F32)


def per_device(inputs, upstream, w_in, bias_in, w_out):
    rows, width = inputs.shape
    scale = 1.0 / math.sqrt(rows * lax.axis_size("dp"))
    any_space = pl.BlockSpec(memory_space=pl.ANY)
    vmem = pl.BlockSpec(memory_space=pltpu.VMEM)
    shard = (SH, FC)
    ring = (NZ,) + shard
    acc = (2, ROWS, FC)
    turned = (NZ, 2, SH, ROWS)
    dx, parts_i, parts_o = pl.pallas_call(
        lambda *refs: kernel(scale, *refs),
        out_shape=(
            jax.ShapeDtypeStruct((SH, ROWS), BF16),
            jax.ShapeDtypeStruct((3,) + shard, BF16),
            jax.ShapeDtypeStruct((3,) + shard, BF16),
        ),
        in_specs=[any_space, any_space, any_space, any_space, vmem],
        out_specs=(any_space, any_space, any_space),
        scratch_shapes=[
            pltpu.VMEM((SH, ROWS), BF16),
            pltpu.VMEM((rows, width), BF16),
            pltpu.VMEM((rows, width), BF16),
            pltpu.VMEM(turned, BF16),
            pltpu.VMEM(turned, BF16),
            pltpu.VMEM(ring, BF16),
            pltpu.VMEM(ring, BF16),
            pltpu.VMEM(acc, F32),
            pltpu.VMEM(acc, F32),
            pltpu.VMEM(acc, BF16),
            pltpu.VMEM(acc, F32),
            pltpu.VMEM(acc, F32),
            pltpu.VMEM(acc, BF16),
            pltpu.VMEM(acc, F32),
            pltpu.VMEM(ring, BF16),
            pltpu.VMEM(ring, BF16),
            pltpu.VMEM((4,) + shard, BF16),
            pltpu.VMEM((4,) + shard, BF16),
            pltpu.VMEM((4,) + shard, BF16),
            pltpu.VMEM((4,) + shard, BF16),
            pltpu.VMEM((4, 4, HF, ROWS), BF16),
            pltpu.VMEM((4, 4, HF, ROWS), BF16),
            pltpu.VMEM((4, HF, ROWS), BF16),
            pltpu.VMEM((4, HF, ROWS), BF16),
            pltpu.VMEM((3, 4, HF, ROWS), BF16),
            pltpu.VMEM((3, 4, HF, ROWS), BF16),
            pltpu.VMEM((3, HF, ROWS), BF16),
            pltpu.VMEM((3, HF, ROWS), BF16),
            pltpu.VMEM((HF, ROWS), BF16),
            pltpu.VMEM((2, 8, FC), F32),
            pltpu.SemaphoreType.DMA((5,)),
            pltpu.SemaphoreType.DMA((4,)),
            pltpu.SemaphoreType.DMA((4,)),
            pltpu.SemaphoreType.DMA((32,)),
            pltpu.SemaphoreType.DMA((32,)),
            pltpu.SemaphoreType.DMA((16,)),
            pltpu.SemaphoreType.DMA((16,)),
            pltpu.SemaphoreType.DMA((4,)),
            pltpu.SemaphoreType.DMA((4,)),
            pltpu.SemaphoreType.DMA((32,)),
            pltpu.SemaphoreType.DMA((32,)),
            pltpu.SemaphoreType.DMA((4,)),
            pltpu.SemaphoreType.DMA((12,)),
            pltpu.SemaphoreType.DMA((12,)),
            pltpu.SemaphoreType.DMA((12,)),
        ],
        compiler_params=pltpu.CompilerParams(
            collective_id=0, has_side_effects=True, vmem_limit_bytes=60 * 1024 * 1024
        ),
    )(inputs, upstream, w_in, w_out.T, bias_in)
    steps = 2
    part_spec = pl.BlockSpec((3, SH // steps, FC), lambda i: (0, i, 0))
    dx_spec = pl.BlockSpec((SH // steps, ROWS), lambda i: (i, 0))
    dw_spec = pl.BlockSpec((SH // steps, FC), lambda i: (i, 0))
    dx, dwin, dwout = pl.pallas_call(
        finish,
        grid=(steps,),
        out_shape=(
            jax.ShapeDtypeStruct((SH, ROWS), BF16),
            jax.ShapeDtypeStruct(shard, F32),
            jax.ShapeDtypeStruct(shard, F32),
        ),
        in_specs=[dx_spec, part_spec, part_spec],
        out_specs=(dx_spec, dw_spec, dw_spec),
    )(dx, parts_i, parts_o)
    return dx.T, dwin, dwout.T


def solution(mesh):
    placed = (P("dp", None), P("dp", None), P("dp", "tensor"), P("tensor"), P("tensor", "dp"))
    return jax.shard_map(
        per_device,
        mesh=mesh,
        in_specs=placed,
        out_specs=(P("dp", "tensor"), P("dp", "tensor"), P("tensor", "dp")),
        check_vma=False,
    )
```

```python
import math

import jax
import jax.numpy as jnp
from jax import lax
from jax.experimental import pallas as pl
from jax.experimental.pallas import tpu as pltpu
from jax.sharding import PartitionSpec as P

MESH = pl.DeviceIdType.MESH
ROOT_HALF = 0.7071067811865476
INV_ROOT_TWO_PI = 0.3989422804014327
BF16 = jnp.bfloat16
F32 = jnp.float32

NZ = 8
NT = 8
ROWS = 256
SH = 320
HF = SH // 2
QD = SH // 4
QR = ROWS // 2
FC = 640
PARTS = (pl.ds(0, HF), pl.ds(HF, HF))

TN = (((0,), (0,)), ((), ()))
NN = (((1,), (0,)), ((), ()))
NT_DIMS = (((1,), (1,)), ((), ()))


def dot(lhs, rhs, dims):
    return lax.dot_general(lhs, rhs, dims, preferred_element_type=F32)


def kernel(
    scale, x_hbm, dy_hbm, win_hbm, wout_hbm, bias_ref,
    dx_out, parts_i, parts_o,
    dx_v, xv, dyv, tv, xt, dyt, wi, wo,
    pre, pre_in, act, gp, slope,
    term_g, term_i, rin_g, rin_i, lin_g, lin_i, dwo, dwo_in, dwo_v,
    dxa, dxb, sum_a, sum_b, in_a, in_b, last_a, last_b, turn_v, bias_in,
    ld_sem, sw_s, sw_r, ag_s, ag_r, ex_s, ex_r, core_s, core_r,
    rs_s, rs_r, own_s, own_r, dx_s, dx_r, dz_s, dz_r, dy_s, dy_r,
):
    dp = lax.axis_index("dp")
    tn = lax.axis_index("tensor")
    z, a = lax.div(dp, 2), lax.rem(dp, 2)
    t2, b = lax.div(tn, 2), lax.rem(tn, 2)
    x_, ypar = lax.div(t2, 2), lax.rem(t2, 2)
    y_ = 2 * a + ypar
    same = a == b
    differ = a != b
    zr, zl = lax.rem(z + 1, NZ), lax.rem(z + NZ - 1, NZ)

    def dev(z_, t_, a_, b_):
        return {"dp": 2 * z_ + a_, "tensor": 2 * t_ + b_}

    right, left = dev(zr, t2, a, b), dev(zl, t2, a, b)
    other_core = dev(z, t2, a, 1 - b)
    y_side = dev(z, t2 + 1 - 2 * ypar, 1 - a, b)

    def x_peer(r):
        return lax.rem(x_ + r, 4)

    def y_peer(r):
        yy = lax.rem(y_ + r, 4)
        return lax.rem(yy, 2), lax.div(yy, 2)

    def x_dev(r):
        return dev(z, 2 * x_peer(r) + ypar, a, b)

    def y_dev(r):
        yl, ah = y_peer(r)
        return dev(z, 2 * x_ + yl, ah, b)

    def rc(src, dst, ss, rs, to):
        return pltpu.make_async_remote_copy(
            src_ref=src, dst_ref=dst, send_sem=ss, recv_sem=rs, device_id=to, device_id_type=MESH
        )

    def part_rows(p):
        if isinstance(p, int):
            return PARTS[p]
        return pl.ds(pl.multiple_of(p * HF, HF), HF)

    hbm = (win_hbm, wout_hbm)
    weights = (wi, wo)
    here = part_rows(b)

    def ld_w(w):
        return pltpu.make_async_copy(hbm[w].at[here], weights[w].at[(0, b)[w], part_rows(a)], ld_sem.at[2 + w])

    ld_x = pltpu.make_async_copy(x_hbm, xv, ld_sem.at[0])
    ld_dy = pltpu.make_async_copy(dy_hbm, dyv, ld_sem.at[1])
    put_dx = pltpu.make_async_copy(dx_v, dx_out, ld_sem.at[4])

    @pl.when(same)
    def _():
        ld_w(0).start()
        ld_w(1).start()

    pl.when(same)(ld_dy.start)
    ld_x.start()

    barrier = pltpu.get_barrier_semaphore()

    def greet(to):
        pl.semaphore_signal(barrier, inc=1, device_id=to, device_id_type=MESH)

    for z_ in (zr, zl):
        greet(dev(z_, t2, a, b))
        greet(dev(z_, t2, a, 1 - b))
    for d in range(2, 7):
        greet(dev(lax.rem(z + d, NZ), t2, a, b))
    greet(other_core)
    greet(dev(z, t2, 1 - a, b))
    greet(dev(z, t2, 1 - a, 1 - b))
    for r in (1, 2, 3):
        greet(x_dev(r))
    greet(y_dev(1))
    greet(y_dev(3))
    pl.semaphore_wait(barrier, 17)

    def to_twin(w):
        rows = part_rows(a)
        return rc(hbm[w].at[part_rows(1 - b)], weights[w].at[(0, 1 - b)[w], rows], sw_s.at[2 * w], sw_r.at[2 * w], other_core)

    def to_chip(w, h):
        rows = part_rows(a)
        return rc(
            hbm[w].at[part_rows(h)], weights[w].at[(0, h)[w], rows], sw_s.at[2 * w + h], sw_r.at[2 * w + 1], dev(z, t2, b, h)
        )

    def from_twin(w):
        return rc(hbm[w].at[here], weights[w].at[(0, b)[w], part_rows(a)], sw_s.at[2 * w], sw_r.at[2 * w], other_core)

    def from_chip(w):
        return rc(hbm[w].at[here], weights[w].at[(0, b)[w], part_rows(1 - a)], sw_s.at[2 * w], sw_r.at[2 * w + 1], other_core)

    @pl.when(same)
    def _():
        to_twin(0).start()

    @pl.when(differ)
    def _():
        for h in range(2):
            to_chip(0, h).start()

    gathered = (wi, act)

    def piece(w, part):
        size = (HF, QR)[w]
        if isinstance(part, int):
            return pl.ds(part * size, size)
        return pl.ds(pl.multiple_of(part * size, size), size)

    def ag(w, g, s, part):
        buf, rows = gathered[w], piece(w, part)
        if g == 0:
            src, dst, to = s - 1, s, right
        else:
            src, dst, to = (NZ + 1 - s) % NZ, NZ - s, left
        i = ((w * 2 + g) * 4 + s - 1) * 2 + part
        return rc(buf.at[src, rows], buf.at[dst, rows], ag_s.at[i], ag_r.at[i], to)

    def send_first(part):
        for g in range(2):
            ag(0, g, 1, part).start()

    @pl.when(same)
    def _():
        ld_w(0).wait()

    @pl.when(differ)
    def _():
        from_twin(0).wait_recv()

    send_first(a)

    xh, xq = lax.div(x_, 2), lax.rem(x_, 2)
    cut_rows = pl.ds(pl.multiple_of(SH * xq + HF * xh + QD * ypar, QD), QD)
    FAR, NEAR = pl.ds(4, 4), pl.ds(0, 4)

    def dy_z(d):
        to = dev(lax.rem(z + d, NZ), t2, a, b)
        return rc(tv.at[d, cut_rows], dyt.at[(d + 2) % NZ, xh, xq, ypar], dz_s.at[d], dz_r.at[d], to)

    def dy_msg(kind, r, batch, tail, to):
        m = kind * 3 + r - 1
        ref = dyt.at[(batch,) + tail]
        return rc(ref, ref, dy_s.at[m], dy_r.at[m], to)

    def far_y(r):
        return dy_msg(0, r, FAR, (xh, xq, ypar), y_dev(r))

    def far_y_in(r):
        return dy_msg(0, r, FAR, (xh, xq, lax.rem(y_ + 4 - r, 2)), y_dev(r))

    def far_x(r):
        return dy_msg(1, r, FAR, (xh, xq), x_dev(r))

    def far_x_in(r):
        xs = lax.rem(x_ + 4 - r, 4)
        return dy_msg(1, r, FAR, (lax.div(xs, 2), lax.rem(xs, 2)), x_dev(r))

    def near_x(r):
        return dy_msg(2, r, NEAR, (xh, xq, ypar), x_dev(r))

    def near_x_in(r):
        xs = lax.rem(x_ + 4 - r, 4)
        return dy_msg(2, r, NEAR, (lax.div(xs, 2), lax.rem(xs, 2), ypar), x_dev(r))

    whole = pl.ds(0, 2)

    def near_y(r):
        return dy_msg(3, r, NEAR, (whole, whole, ypar), y_dev(r))

    def near_y_in(r):
        return dy_msg(3, r, NEAR, (whole, whole, lax.rem(y_ + 4 - r, 2)), y_dev(r))

    def from_source(r, wait):
        pl.when(lax.div(lax.rem(y_ + 4 - r, 4), 2) == b)(wait)

    @pl.when(same)
    def _():
        ld_dy.wait()

        def turn_dy(d, carry):
            k = lax.rem(z + d, NZ)
            tv[d] = dyv[:, pl.ds(pl.multiple_of(k * 2 * SH, 128), 2 * SH)].T
            return carry

        lax.fori_loop(0, NZ, turn_dy, 0)
        for d in (4, 3, 5, 2, 6, 1, 7):
            dy_z(d).start()
        dyt[2, xh, xq, ypar] = tv[0, cut_rows]

    bias_in[0] = jnp.broadcast_to(bias_ref[...].astype(F32)[None, :], (8, FC))
    bias_cp = rc(bias_in.at[0], bias_in.at[1], core_s.at[2], core_r.at[2], other_core)
    bias_cp.start()

    quads = ((0, 1, 7, 2), (6, 3, 5, 4))

    def at_x(i, x):
        p, q, r, t = quads[i]
        return jnp.where(x < 2, jnp.where(x == 0, p, q), jnp.where(x == 2, r, t))

    def turn(src, dst, d):
        k = lax.rem(z + NZ - d, NZ)
        v = src[:, pl.ds(pl.multiple_of(k * 2 * SH, 128), 2 * SH)].T
        first = b == 0
        dst[d, a, PARTS[0]] = jnp.where(first, v[:HF], v[HF:SH])
        dst[d, a, PARTS[1]] = jnp.where(first, v[SH : SH + HF], v[SH + HF :])

    def ex_y(i):
        ref = xt.at[at_x(i, x_), a]
        return rc(ref, ref, ex_s.at[i], ex_r.at[i], y_side)

    def ex_y_in(i):
        ref = xt.at[at_x(i, x_), 1 - a]
        return rc(ref, ref, ex_s.at[i], ex_r.at[i], y_side)

    def ex_x(i, r):
        ref, m = xt.at[at_x(i, x_), 1 - a], 1 + 3 * i + r
        return rc(ref, ref, ex_s.at[m], ex_r.at[m], x_dev(r))

    def ex_x_in(i, r):
        ref, m = xt.at[at_x(i, lax.rem(x_ + 4 - r, 4)), 1 - a], 1 + 3 * i + r
        return rc(ref, ref, ex_s.at[m], ex_r.at[m], x_dev(r))

    ld_x.wait()
    for d in range(NZ):
        turn(xv, xt, d)

    from_chip(0).wait_recv()
    send_first(1 - a)

    @pl.when(same)
    def _():
        for d in (4, 3, 5, 2):
            dy_z(d).wait_recv()
        for r in (1, 3, 2):
            far_y(r).start()
        for d in (6, 1, 7):
            dy_z(d).wait_recv()
        for r in (1, 3, 2):
            near_x(r).start()

    def pass_on(i):
        ex_y_in(i).wait_recv()
        for r in (1, 3, 2):
            ex_x(i, r).start()

    def step(w, s, part):
        for g in range(2):
            ag(w, g, s, part).wait_recv()
            ag(w, g, s + 1, part).start()

    def accumulate(acc, src, w, slots, first=False):
        n = len(slots)

        def body(i, carry):
            j, h = lax.div(i, 2), lax.rem(i, 2)
            d = slots[0] if n == 1 else slots[0] + j * (slots[1] - slots[0])
            acc[h] += dot(src[d, h], w[d], TN)
            return carry

        if first:
            acc[...] = jnp.zeros_like(acc)
        lax.fori_loop(0, 2 * n, body, 0)

    firsts = (0, 1)
    seconds = (1, 0)

    terms, rins, lins = (term_g, term_i), (rin_g, rin_i), (lin_g, lin_i)

    def make_terms(w, lo, hi):
        def body(i, carry):
            d = lax.rem(4 + lax.div(i + 1, 2) * (2 * lax.rem(i, 2) - 1) + NZ, NZ)
            if w == 0:
                j = lax.rem(d + 2, NZ)
                total = dot(dyt[j, 0].reshape(SH, ROWS), wo[0], TN) + dot(dyt[j, 1].reshape(SH, ROWS), wo[1], TN)
            else:
                total = (dot(xt[d, 0], gp[0], NN) + dot(xt[d, 1], gp[1], NN)) * scale
            terms[w][d] = total.astype(BF16)
            return carry

        lax.fori_loop(lo, hi, body, 0)

    def rs(w, g, e, part, last=False):
        rows = piece(1 - w, part)
        src = terms[w].at[NZ - e if g == 0 else e, rows]
        i = ((w * 2 + g) * 4 + e - 1) * 2 + part
        if last:
            m = 4 + (w * 2 + g) * 2 + b
            return rc(src, parts_i.at[1 + g, here], rs_s.at[i], own_r.at[m], dev((zr, zl)[g], t2, a, a))
        return rc(src, (rins, lins)[g][w].at[e - 1, rows], rs_s.at[i], rs_r.at[i], (right, left)[g])

    def last_in(w, g, h):
        m = 4 + (w * 2 + g) * 2 + h
        return rc(terms[w].at[0, PARTS[h]], parts_i.at[1 + g, PARTS[h]], own_s.at[0], own_r.at[m], right)

    def hop(w, g, e, part, last=False):
        rs(w, g, e + 1, part).wait_recv()
        d, rows = NZ - e if g == 0 else e, piece(1 - w, part)
        buf, came = terms[w], (rins, lins)[g][w]
        buf[d, rows] = (buf[d, rows].astype(F32) + came[e, rows].astype(F32)).astype(BF16)
        rs(w, g, e, part, last).start()

    def end_src(w, part):
        return dwo_v.at[part_rows(part)] if w == 0 else term_i.at[0, part_rows(part)]

    def end_dst(w, rows):
        return parts_o.at[rows] if w == 0 else parts_i.at[0, rows]

    def end_copy(w, part):
        m = 2 * w + part
        return rc(end_src(w, part), end_dst(w, here), own_s.at[m], own_r.at[2 * w + b], dev(z, t2, part, a))

    def end_local(w):
        return pltpu.make_async_copy(end_src(w, a), end_dst(w, here), own_s.at[2 * w + a])

    def end_in(w, h):
        return rc(end_src(w, h), end_dst(w, PARTS[h]), own_s.at[0], own_r.at[2 * w + h], right)

    def send_own(w):
        @pl.when(same)
        def _():
            end_local(w).start()

        @pl.when(differ)
        def _():
            end_copy(w, a).start()

    def send_sum():
        rows = part_rows(1 - a)
        for g in range(2):
            rs(1, g, 1, 1 - a).wait_recv()
        total = term_i[0, rows].astype(F32)
        for came in (rin_i, lin_i):
            total = total + came[0, rows].astype(F32)
        term_i[0, rows] = total.astype(BF16)
        end_copy(1, 1 - a).start()

    def wait_end(w):
        @pl.when(same)
        def _():
            end_local(w).wait()
            if w == 1:
                for g in range(2):
                    for h in range(2):
                        last_in(1, g, h).wait_recv()

        @pl.when(differ)
        def _():
            end_copy(w, a).wait_send()

        end_copy(w, 1 - a).wait_send()
        for h in range(2):
            @pl.when(jnp.logical_not(same & (b == h)))
            def _():
                end_in(w, h).wait_recv()

    step(0, 1, a)
    for r in (1, 2, 3):
        from_source(r, far_y_in(r).wait_recv)
    for r in (1, 3, 2):
        far_x(r).start()
    for i in range(2):
        ex_y(i).start()

    @pl.when(same)
    def _():
        to_twin(1).start()

    @pl.when(differ)
    def _():
        for h in range(2):
            to_chip(1, h).start()

    step(0, 1, 1 - a)
    for part in (a, 1 - a):
        for g in range(2):
            ag(0, g, 2, part).wait_recv()
    for pick in (firsts, seconds):
        for g in range(2):
            ag(0, g, 3, pick[g]).start()
    pass_on(0)

    @pl.when(same)
    def _():
        for r in (1, 2, 3):
            near_x_in(r).wait_recv()
        for r in (1, 3, 2):
            near_y(r).start()

    @pl.when(same)
    def _():
        ld_w(1).wait()

    @pl.when(differ)
    def _():
        from_twin(1).wait_recv()

    from_chip(1).wait_recv()
    wo_cp = rc(wo.at[b], wo.at[b], core_s.at[1], core_r.at[1], other_core)
    wo_in = rc(wo.at[1 - b], wo.at[1 - b], core_s.at[1], core_r.at[1], other_core)
    wo_cp.start()
    for g in range(2):
        ag(0, g, 3, firsts[g]).wait_recv()
        ag(0, g, 4, firsts[g]).start()
    pass_on(1)
    wo_in.wait_recv()
    for r in (1, 2, 3):
        far_x_in(r).wait_recv()
    make_terms(0, 0, 3)
    for g in range(2):
        rs(0, g, 4, firsts[g]).start()
    for g in range(2):
        rs(0, g, 3, seconds[g]).start()
    for r in (1, 2, 3):
        ex_x_in(0, r).wait_recv()
    accumulate(pre, xt, wi, (0,), True)
    accumulate(pre, xt, wi, (1, 7))
    accumulate(pre, xt, wi, (2,))
    for g in range(2):
        hop(0, g, 3, firsts[g])
    for g in range(2):
        ag(0, g, 3, seconds[g]).wait_recv()
    for r in (1, 2, 3):
        ex_x_in(1, r).wait_recv()
    accumulate(pre, xt, wi, (6,))
    accumulate(pre, xt, wi, (3, 5))
    for g in range(2):
        ag(0, g, 4, firsts[g]).wait_recv()
    accumulate(pre, xt, wi, (4,))
    pre_cp = rc(pre.at[1 - b], pre_in, core_s.at[0], core_r.at[0], other_core)
    pre_cp.start()
    for r in (1, 2, 3):
        from_source(r, near_y_in(r).wait_recv)
    make_terms(0, 3, 5)
    for g in range(2):
        hop(0, g, 2, seconds[g])
    bias_cp.wait_recv()
    bias = jnp.where(same, bias_in[0], bias_in[1])[0:1]
    pre_cp.wait_recv()

    def gelu(i, carry):
        rows = pl.ds(pl.multiple_of(i * 32, 32), 32)
        v = pre[b, rows] + pre_in[rows] + bias
        cdf = 0.5 * (1.0 + lax.erf(v * ROOT_HALF))
        act[0, rows] = (v * cdf).astype(BF16)
        slope[rows] = cdf + v * jnp.exp(-0.5 * v * v) * INV_ROOT_TWO_PI
        return carry

    lax.fori_loop(0, 8, gelu, 0)

    for pick in (firsts, seconds):
        for g in range(2):
            ag(1, g, 1, pick[g]).start()
    for g in range(2):
        hop(0, g, 2, firsts[g])
    make_terms(0, 5, 8)

    def add_out(slots, first=False):
        n = len(slots)

        def body(i, carry):
            q, h = lax.div(i, 2), lax.rem(i, 2)
            d = slots[0] if n == 1 else slots[0] + q * (slots[1] - slots[0])
            j = (slots[0] + 2) % NZ if n == 1 else lax.rem(d + 2, NZ)
            dwo[h] += dot(dyt[j, h].reshape(SH, ROWS), act[d], NN)
            return carry

        if first:
            dwo[...] = jnp.zeros_like(dwo)
        lax.fori_loop(0, 2 * n, body, 0)

    def pass_act(s, picks):
        for pick in picks:
            for g in range(2):
                ag(1, g, s, pick[g]).wait_recv()
                ag(1, g, s + 1, pick[g]).start()

    pass_act(1, (firsts, seconds))
    for pick in (seconds, firsts):
        for g in range(2):
            hop(0, g, 1, pick[g])
    add_out((0,), True)
    add_out((1, 7))
    pass_act(2, (firsts, seconds))
    add_out((2, 6))
    for pick in (seconds, firsts):
        for g in range(2):
            rs(0, g, 1, pick[g]).wait_recv()

    def grad(i, carry):
        rows = pl.ds(pl.multiple_of(i * 32, 32), 32)
        v = term_g[0, rows].astype(F32) + rin_g[0, rows].astype(F32) + lin_g[0, rows].astype(F32)
        gp[b, rows] = (v * slope[rows]).astype(BF16)
        return carry

    lax.fori_loop(0, 8, grad, 0)
    gp_cp = rc(gp.at[b], gp.at[b], core_s.at[4], core_r.at[4], other_core)
    gp_cp.start()
    rc(gp.at[1 - b], gp.at[1 - b], core_s.at[4], core_r.at[4], other_core).wait_recv()
    make_terms(1, 0, 3)
    for g in range(2):
        rs(1, g, 4, firsts[g]).start()
    for g in range(2):
        rs(1, g, 3, seconds[g]).start()

    def dx_body(i, carry):
        k, h = lax.div(i, 2), lax.rem(i, 2)
        d = lax.rem(z + NZ - k, NZ)
        v = dot(wi[d], gp[h], NT_DIMS).astype(BF16)
        xx, yy = lax.div(k, 2), 2 * lax.rem(k, 2) + h
        dxa[xx, yy] = v[:HF]
        dxb[yy, xx] = v[HF:]
        return carry

    lax.fori_loop(0, 16, dx_body, 0)
    yy_ = 2 * ypar + a

    def y_index(r):
        yl, ah = y_peer(r)
        return 2 * yl + ah

    def first_a(r):
        return rc(dxa.at[x_peer(r)], in_a.at[r - 1], dx_s.at[r - 1], dx_r.at[r - 1], x_dev(r))

    def first_b(r):
        return rc(dxb.at[y_index(r)], in_b.at[r - 1], dx_s.at[r + 2], dx_r.at[r + 2], y_dev(r))

    def second_a(r):
        return rc(sum_a.at[y_index(r)], last_a.at[r - 1], dx_s.at[r + 5], dx_r.at[r + 5], y_dev(r))

    def second_b(r):
        return rc(sum_b.at[x_peer(r)], last_b.at[r - 1], dx_s.at[r + 8], dx_r.at[r + 8], x_dev(r))

    for r in (1, 2, 3):
        first_a(r).start()
        first_b(r).start()

    for g in range(2):
        hop(1, g, 3, firsts[g])
    pass_act(3, (firsts,))
    make_terms(1, 3, 8)
    send_own(1)
    for part in (1 - a, a):
        for g in range(2):
            hop(1, g, 2, part)

    for g in range(2):
        ag(1, g, 3, seconds[g]).wait_recv()
    add_out((3, 5))
    for g in range(2):
        ag(1, g, 4, firsts[g]).wait_recv()
    add_out((4,))
    dwo_cp = rc(dwo.at[1 - b], dwo_in, core_s.at[5], core_r.at[5], other_core)
    dwo_cp.start()
    for g in range(2):
        hop(1, g, 1, 1 - a)
    dwo_cp.wait_recv()
    dwo_v[...] = ((dwo[b] + dwo_in[...]) * scale).astype(BF16)
    send_own(0)
    end_copy(0, 1 - a).start()

    for r in (1, 2, 3):
        first_a(r).wait_recv()
        first_b(r).wait_recv()

    def sum_body(i, carry):
        total_a, total_b = dxa[x_, i].astype(F32), dxb[yy_, i].astype(F32)
        for r in range(3):
            total_a = total_a + in_a[r, i].astype(F32)
            total_b = total_b + in_b[r, i].astype(F32)
        sum_a[i], sum_b[i] = total_a.astype(BF16), total_b.astype(BF16)
        return carry

    lax.fori_loop(0, 4, sum_body, 0)
    for r in (1, 2, 3):
        second_a(r).start()
        second_b(r).start()

    for g in range(2):
        hop(1, g, 1, a, True)
    send_sum()

    for r in (1, 2, 3):
        second_a(r).wait_recv()
        second_b(r).wait_recv()
    total_a, total_b = sum_a[yy_].astype(F32), sum_b[x_].astype(F32)
    for r in range(3):
        total_a = total_a + last_a[r].astype(F32)
        total_b = total_b + last_b[r].astype(F32)
    total_a, total_b = total_a.astype(BF16), total_b.astype(BF16)
    dx_v[here] = jnp.where(b == 0, total_a, total_b)
    turn_v[...] = jnp.where(b == 0, total_b, total_a)
    dx_cp = rc(turn_v, dx_v.at[here], core_s.at[3], core_r.at[3], other_core)
    dx_cp.start()

    rc(turn_v, dx_v.at[part_rows(1 - b)], core_s.at[3], core_r.at[3], other_core).wait_recv()
    put_dx.start()


    @pl.when(same)
    def _():
        to_twin(0).wait_send()
        to_twin(1).wait_send()

    @pl.when(differ)
    def _():
        for w in range(2):
            for h in range(2):
                to_chip(w, h).wait_send()

    for w in range(2):
        for g in range(2):
            for s in (1, 2, 3):
                for part in range(2):
                    ag(w, g, s, part).wait_send()
            ag(w, g, 4, firsts[g]).wait_send()
    for i in range(2):
        ex_y(i).wait_send()
        for r in (1, 2, 3):
            ex_x(i, r).wait_send()
    for r in (1, 2, 3):
        far_x(r).wait_send()

    @pl.when(same)
    def _():
        for d in range(1, NZ):
            dy_z(d).wait_send()
        for r in (1, 2, 3):
            far_y(r).wait_send()
            near_x(r).wait_send()
            near_y(r).wait_send()

    for cp in (bias_cp, pre_cp, wo_cp, gp_cp, dwo_cp):
        cp.wait_send()
    for w in range(2):
        for g in range(2):
            rs(w, g, 4, firsts[g]).wait_send()
            for e in (3, 2) if w else (3, 2, 1):
                for part in range(2):
                    rs(w, g, e, part).wait_send()
    for r in (1, 2, 3):
        for cp in (first_a(r), first_b(r), second_a(r), second_b(r)):
            cp.wait_send()

    wait_end(0)
    wait_end(1)
    for g in range(2):
        for part in range(2):
            rs(1, g, 1, part).wait_send()
    dx_cp.wait_send()
    put_dx.wait()


def finish(dx_ref, in_ref, out_ref, dx_out, dwin_out, dwout_out):
    dx_out[...] = dx_ref[...]
    whole = lax.rem(lax.axis_index("dp"), 2) != lax.rem(lax.axis_index("tensor"), 2)
    dwout_out[...] = out_ref[...].astype(F32)

    @pl.when(whole)
    def _():
        dwin_out[...] = in_ref[0].astype(F32)

    @pl.when(jnp.logical_not(whole))
    def _():
        dwin_out[...] = in_ref[0].astype(F32) + in_ref[1].astype(F32) + in_ref[2].astype(F32)


def per_device(inputs, upstream, w_in, bias_in, w_out):
    rows, width = inputs.shape
    scale = 1.0 / math.sqrt(rows * lax.axis_size("dp"))
    any_space = pl.BlockSpec(memory_space=pl.ANY)
    vmem = pl.BlockSpec(memory_space=pltpu.VMEM)
    shard = (SH, FC)
    ring = (NZ,) + shard
    acc = (2, ROWS, FC)
    half = (ROWS, FC)
    turned = (NZ, 2, SH, ROWS)
    dx, parts_i, parts_o = pl.pallas_call(
        lambda *refs: kernel(scale, *refs),
        out_shape=(
            jax.ShapeDtypeStruct((SH, ROWS), BF16),
            jax.ShapeDtypeStruct((3,) + shard, BF16),
            jax.ShapeDtypeStruct(shard, BF16),
        ),
        in_specs=[any_space, any_space, any_space, any_space, vmem],
        out_specs=(any_space, any_space, any_space),
        scratch_shapes=[
            pltpu.VMEM((SH, ROWS), BF16),
            pltpu.VMEM((rows, width), BF16),
            pltpu.VMEM((rows, width), BF16),
            pltpu.VMEM((NZ, 2 * SH, ROWS), BF16),
            pltpu.VMEM(turned, BF16),
            pltpu.VMEM((NZ, 2, 2, 2, QD, ROWS), BF16),
            pltpu.VMEM(ring, BF16),
            pltpu.VMEM((2,) + shard, BF16),
            pltpu.VMEM(acc, F32),
            pltpu.VMEM(half, F32),
            pltpu.VMEM((NZ,) + half, BF16),
            pltpu.VMEM(acc, BF16),
            pltpu.VMEM(half, F32),
            pltpu.VMEM((NZ,) + half, BF16),
            pltpu.VMEM(ring, BF16),
            pltpu.VMEM((4,) + half, BF16),
            pltpu.VMEM((4,) + shard, BF16),
            pltpu.VMEM((4,) + half, BF16),
            pltpu.VMEM((4,) + shard, BF16),
            pltpu.VMEM((2,) + shard, F32),
            pltpu.VMEM(shard, F32),
            pltpu.VMEM(shard, BF16),
            pltpu.VMEM((4, 4, HF, ROWS), BF16),
            pltpu.VMEM((4, 4, HF, ROWS), BF16),
            pltpu.VMEM((4, HF, ROWS), BF16),
            pltpu.VMEM((4, HF, ROWS), BF16),
            pltpu.VMEM((3, 4, HF, ROWS), BF16),
            pltpu.VMEM((3, 4, HF, ROWS), BF16),
            pltpu.VMEM((3, HF, ROWS), BF16),
            pltpu.VMEM((3, HF, ROWS), BF16),
            pltpu.VMEM((HF, ROWS), BF16),
            pltpu.VMEM((2, 8, FC), F32),
            pltpu.SemaphoreType.DMA((5,)),
            pltpu.SemaphoreType.DMA((4,)),
            pltpu.SemaphoreType.DMA((4,)),
            pltpu.SemaphoreType.DMA((32,)),
            pltpu.SemaphoreType.DMA((32,)),
            pltpu.SemaphoreType.DMA((16,)),
            pltpu.SemaphoreType.DMA((16,)),
            pltpu.SemaphoreType.DMA((6,)),
            pltpu.SemaphoreType.DMA((6,)),
            pltpu.SemaphoreType.DMA((32,)),
            pltpu.SemaphoreType.DMA((32,)),
            pltpu.SemaphoreType.DMA((4,)),
            pltpu.SemaphoreType.DMA((12,)),
            pltpu.SemaphoreType.DMA((12,)),
            pltpu.SemaphoreType.DMA((12,)),
            pltpu.SemaphoreType.DMA((8,)),
            pltpu.SemaphoreType.DMA((8,)),
            pltpu.SemaphoreType.DMA((12,)),
            pltpu.SemaphoreType.DMA((12,)),
        ],
        compiler_params=pltpu.CompilerParams(
            collective_id=0, has_side_effects=True, vmem_limit_bytes=60 * 1024 * 1024
        ),
    )(inputs, upstream, w_in, w_out.T, bias_in)
    steps = 2
    part_spec = pl.BlockSpec((3, SH // steps, FC), lambda i: (0, i, 0))
    dx_spec = pl.BlockSpec((SH // steps, ROWS), lambda i: (i, 0))
    dw_spec = pl.BlockSpec((SH // steps, FC), lambda i: (i, 0))
    dx, dwin, dwout = pl.pallas_call(
        finish,
        grid=(steps,),
        out_shape=(
            jax.ShapeDtypeStruct((SH, ROWS), BF16),
            jax.ShapeDtypeStruct(shard, F32),
            jax.ShapeDtypeStruct(shard, F32),
        ),
        in_specs=[dx_spec, part_spec, dw_spec],
        out_specs=(dx_spec, dw_spec, dw_spec),
    )(dx, parts_i, parts_o)
    return dx.T, dwin, dwout.T


def solution(mesh):
    placed = (P("dp", None), P("dp", None), P("dp", "tensor"), P("tensor"), P("tensor", "dp"))
    return jax.shard_map(
        per_device,
        mesh=mesh,
        in_specs=placed,
        out_specs=(P("dp", "tensor"), P("dp", "tensor"), P("tensor", "dp")),
        check_vma=False,
    )
```

```python
import math

import jax
import jax.numpy as jnp
from jax import lax
from jax.experimental import pallas as pl
from jax.experimental.pallas import tpu as pltpu
from jax.sharding import PartitionSpec as P

MESH = pl.DeviceIdType.MESH
ROOT_HALF = 0.7071067811865476
INV_ROOT_TWO_PI = 0.3989422804014327
BF16 = jnp.bfloat16
F32 = jnp.float32

NZ = 8
NT = 8
ROWS = 256
SH = 320
HF = SH // 2
QD = SH // 4
QR = ROWS // 2
FC = 640
PARTS = (pl.ds(0, HF), pl.ds(HF, HF))

TN = (((0,), (0,)), ((), ()))
NN = (((1,), (0,)), ((), ()))
NT_DIMS = (((1,), (1,)), ((), ()))


def dot(lhs, rhs, dims):
    return lax.dot_general(lhs, rhs, dims, preferred_element_type=F32)


def kernel(
    scale, x_hbm, dy_hbm, win_hbm, wout_hbm, bias_ref,
    dx_out, parts_i, parts_o,
    dx_v, xv, dyv, tv, xt, dyt, wi, wo,
    pre, pre_in, act, gp, slope,
    term_g, term_i, rin_g, rin_i, lin_g, lin_i, dwo, dwo_in, dwo_v,
    dxa, dxb, sum_a, sum_b, in_a, in_b, last_a, last_b, turn_v, bias_in,
    ld_sem, sw_s, sw_r, ag_s, ag_r, ex_s, ex_r, core_s, core_r,
    rs_s, rs_r, own_s, own_r, dx_s, dx_r, dz_s, dz_r, dy_s, dy_r,
):
    dp = lax.axis_index("dp")
    tn = lax.axis_index("tensor")
    z, a = lax.div(dp, 2), lax.rem(dp, 2)
    t2, b = lax.div(tn, 2), lax.rem(tn, 2)
    x_, ypar = lax.div(t2, 2), lax.rem(t2, 2)
    y_ = 2 * a + ypar
    same = a == b
    differ = a != b
    zr, zl = lax.rem(z + 1, NZ), lax.rem(z + NZ - 1, NZ)

    def dev(z_, t_, a_, b_):
        return {"dp": 2 * z_ + a_, "tensor": 2 * t_ + b_}

    right, left = dev(zr, t2, a, b), dev(zl, t2, a, b)
    other_core = dev(z, t2, a, 1 - b)
    y_side = dev(z, t2 + 1 - 2 * ypar, 1 - a, b)

    def x_peer(r):
        return lax.rem(x_ + r, 4)

    def y_peer(r):
        yy = lax.rem(y_ + r, 4)
        return lax.rem(yy, 2), lax.div(yy, 2)

    def x_dev(r):
        return dev(z, 2 * x_peer(r) + ypar, a, b)

    def y_dev(r):
        yl, ah = y_peer(r)
        return dev(z, 2 * x_ + yl, ah, b)

    def rc(src, dst, ss, rs, to):
        return pltpu.make_async_remote_copy(
            src_ref=src, dst_ref=dst, send_sem=ss, recv_sem=rs, device_id=to, device_id_type=MESH
        )

    def part_rows(p):
        if isinstance(p, int):
            return PARTS[p]
        return pl.ds(pl.multiple_of(p * HF, HF), HF)

    hbm = (win_hbm, wout_hbm)
    weights = (wi, wo)
    here = part_rows(b)

    def ld_w(w):
        return pltpu.make_async_copy(hbm[w].at[here], weights[w].at[(0, b)[w], part_rows(a)], ld_sem.at[2 + w])

    ld_x = pltpu.make_async_copy(x_hbm, xv, ld_sem.at[0])
    ld_dy = pltpu.make_async_copy(dy_hbm, dyv, ld_sem.at[1])
    put_dx = pltpu.make_async_copy(dx_v, dx_out, ld_sem.at[4])

    @pl.when(same)
    def _():
        ld_w(0).start()
        ld_w(1).start()

    pl.when(same)(ld_dy.start)
    ld_x.start()

    barrier = pltpu.get_barrier_semaphore()

    def greet(to):
        pl.semaphore_signal(barrier, inc=1, device_id=to, device_id_type=MESH)

    for z_ in (zr, zl):
        greet(dev(z_, t2, a, b))
        greet(dev(z_, t2, a, 1 - b))
    for d in range(2, 7):
        greet(dev(lax.rem(z + d, NZ), t2, a, b))
    greet(other_core)
    greet(dev(z, t2, 1 - a, b))
    greet(dev(z, t2, 1 - a, 1 - b))
    for r in (1, 2, 3):
        greet(x_dev(r))
    greet(y_dev(1))
    greet(y_dev(3))
    pl.semaphore_wait(barrier, 17)

    def to_twin(w):
        rows = part_rows(a)
        return rc(hbm[w].at[part_rows(1 - b)], weights[w].at[(0, 1 - b)[w], rows], sw_s.at[2 * w], sw_r.at[2 * w], other_core)

    def to_chip(w, h):
        rows = part_rows(a)
        return rc(
            hbm[w].at[part_rows(h)], weights[w].at[(0, h)[w], rows], sw_s.at[2 * w + h], sw_r.at[2 * w + 1], dev(z, t2, b, h)
        )

    def from_twin(w):
        return rc(hbm[w].at[here], weights[w].at[(0, b)[w], part_rows(a)], sw_s.at[2 * w], sw_r.at[2 * w], other_core)

    def from_chip(w):
        return rc(hbm[w].at[here], weights[w].at[(0, b)[w], part_rows(1 - a)], sw_s.at[2 * w], sw_r.at[2 * w + 1], other_core)

    @pl.when(same)
    def _():
        to_twin(0).start()

    @pl.when(differ)
    def _():
        for h in range(2):
            to_chip(0, h).start()

    gathered = (wi, act)

    def piece(w, part):
        size = (HF, QR)[w]
        if isinstance(part, int):
            return pl.ds(part * size, size)
        return pl.ds(pl.multiple_of(part * size, size), size)

    def ag(w, g, s, part):
        buf, rows = gathered[w], piece(w, part)
        if g == 0:
            src, dst, to = s - 1, s, right
        else:
            src, dst, to = (NZ + 1 - s) % NZ, NZ - s, left
        i = ((w * 2 + g) * 4 + s - 1) * 2 + part
        return rc(buf.at[src, rows], buf.at[dst, rows], ag_s.at[i], ag_r.at[i], to)

    def send_first(part):
        for g in range(2):
            ag(0, g, 1, part).start()

    @pl.when(same)
    def _():
        ld_w(0).wait()

    @pl.when(differ)
    def _():
        from_twin(0).wait_recv()

    send_first(a)

    xh, xq = lax.div(x_, 2), lax.rem(x_, 2)
    cut_rows = pl.ds(pl.multiple_of(SH * xq + HF * xh + QD * ypar, QD), QD)
    FAR, NEAR = pl.ds(4, 4), pl.ds(0, 4)

    def dy_z(d):
        to = dev(lax.rem(z + d, NZ), t2, a, b)
        return rc(tv.at[d, cut_rows], dyt.at[(d + 2) % NZ, xh, xq, ypar], dz_s.at[d], dz_r.at[d], to)

    def dy_msg(kind, r, batch, tail, to):
        m = kind * 3 + r - 1
        ref = dyt.at[(batch,) + tail]
        return rc(ref, ref, dy_s.at[m], dy_r.at[m], to)

    def far_y(r):
        return dy_msg(0, r, FAR, (xh, xq, ypar), y_dev(r))

    def far_y_in(r):
        return dy_msg(0, r, FAR, (xh, xq, lax.rem(y_ + 4 - r, 2)), y_dev(r))

    def far_x(r):
        return dy_msg(1, r, FAR, (xh, xq), x_dev(r))

    def far_x_in(r):
        xs = lax.rem(x_ + 4 - r, 4)
        return dy_msg(1, r, FAR, (lax.div(xs, 2), lax.rem(xs, 2)), x_dev(r))

    def near_x(r):
        return dy_msg(2, r, NEAR, (xh, xq, ypar), x_dev(r))

    def near_x_in(r):
        xs = lax.rem(x_ + 4 - r, 4)
        return dy_msg(2, r, NEAR, (lax.div(xs, 2), lax.rem(xs, 2), ypar), x_dev(r))

    whole = pl.ds(0, 2)

    def near_y(r):
        return dy_msg(3, r, NEAR, (whole, whole, ypar), y_dev(r))

    def near_y_in(r):
        return dy_msg(3, r, NEAR, (whole, whole, lax.rem(y_ + 4 - r, 2)), y_dev(r))

    def from_source(r, wait):
        pl.when(lax.div(lax.rem(y_ + 4 - r, 4), 2) == b)(wait)

    @pl.when(same)
    def _():
        ld_dy.wait()

        def turn_dy(d, carry):
            k = lax.rem(z + d, NZ)
            tv[d] = dyv[:, pl.ds(pl.multiple_of(k * 2 * SH, 128), 2 * SH)].T
            return carry

        lax.fori_loop(0, NZ, turn_dy, 0)
        for d in (4, 3, 5, 2, 6, 1, 7):
            dy_z(d).start()
        dyt[2, xh, xq, ypar] = tv[0, cut_rows]

    bias_in[0] = jnp.broadcast_to(bias_ref[...].astype(F32)[None, :], (8, FC))
    bias_cp = rc(bias_in.at[0], bias_in.at[1], core_s.at[2], core_r.at[2], other_core)
    bias_cp.start()

    quads = ((0, 1, 7, 2), (6, 3, 5, 4))

    def at_x(i, x):
        p, q, r, t = quads[i]
        return jnp.where(x < 2, jnp.where(x == 0, p, q), jnp.where(x == 2, r, t))

    def turn(src, dst, d):
        k = lax.rem(z + NZ - d, NZ)
        v = src[:, pl.ds(pl.multiple_of(k * 2 * SH, 128), 2 * SH)].T
        first = b == 0
        dst[d, a, PARTS[0]] = jnp.where(first, v[:HF], v[HF:SH])
        dst[d, a, PARTS[1]] = jnp.where(first, v[SH : SH + HF], v[SH + HF :])

    def ex_y(i):
        ref = xt.at[at_x(i, x_), a]
        return rc(ref, ref, ex_s.at[i], ex_r.at[i], y_side)

    def ex_y_in(i):
        ref = xt.at[at_x(i, x_), 1 - a]
        return rc(ref, ref, ex_s.at[i], ex_r.at[i], y_side)

    def ex_x(i, r):
        ref, m = xt.at[at_x(i, x_), 1 - a], 1 + 3 * i + r
        return rc(ref, ref, ex_s.at[m], ex_r.at[m], x_dev(r))

    def ex_x_in(i, r):
        ref, m = xt.at[at_x(i, lax.rem(x_ + 4 - r, 4)), 1 - a], 1 + 3 * i + r
        return rc(ref, ref, ex_s.at[m], ex_r.at[m], x_dev(r))

    ld_x.wait()
    for d in range(NZ):
        turn(xv, xt, d)

    from_chip(0).wait_recv()
    send_first(1 - a)

    @pl.when(same)
    def _():
        for d in (4, 3, 5, 2):
            dy_z(d).wait_recv()
        for r in (1, 3, 2):
            far_y(r).start()
        for d in (6, 1, 7):
            dy_z(d).wait_recv()
        for r in (1, 3, 2):
            near_x(r).start()

    def pass_on(i):
        ex_y_in(i).wait_recv()
        for r in (1, 3, 2):
            ex_x(i, r).start()

    def step(w, s, part):
        for g in range(2):
            ag(w, g, s, part).wait_recv()
            ag(w, g, s + 1, part).start()

    def accumulate(acc, src, w, slots, first=False):
        n = len(slots)

        def body(i, carry):
            j, h = lax.div(i, 2), lax.rem(i, 2)
            d = slots[0] if n == 1 else slots[0] + j * (slots[1] - slots[0])
            acc[h] += dot(src[d, h], w[d], TN)
            return carry

        if first:
            acc[...] = jnp.zeros_like(acc)
        lax.fori_loop(0, 2 * n, body, 0)

    firsts = (0, 1)
    seconds = (1, 0)

    terms, rins, lins = (term_g, term_i), (rin_g, rin_i), (lin_g, lin_i)

    def make_terms(w, lo, hi):
        def body(i, carry):
            d = lax.rem(4 + lax.div(i + 1, 2) * (2 * lax.rem(i, 2) - 1) + NZ, NZ)
            if w == 0:
                j = lax.rem(d + 2, NZ)
                total = dot(dyt[j, 0].reshape(SH, ROWS), wo[0], TN) + dot(dyt[j, 1].reshape(SH, ROWS), wo[1], TN)
            else:
                total = (dot(xt[d, 0], gp[0], NN) + dot(xt[d, 1], gp[1], NN)) * scale
            terms[w][d] = total.astype(BF16)
            return carry

        lax.fori_loop(lo, hi, body, 0)

    def rs(w, g, e, part, last=False):
        rows = piece(1 - w, part)
        src = terms[w].at[NZ - e if g == 0 else e, rows]
        i = ((w * 2 + g) * 4 + e - 1) * 2 + part
        if last:
            m = 4 + (w * 2 + g) * 2 + b
            return rc(src, parts_i.at[1 + g, here], rs_s.at[i], own_r.at[m], dev((zr, zl)[g], t2, a, a))
        return rc(src, (rins, lins)[g][w].at[e - 1, rows], rs_s.at[i], rs_r.at[i], (right, left)[g])

    def last_in(w, g, h):
        m = 4 + (w * 2 + g) * 2 + h
        return rc(terms[w].at[0, PARTS[h]], parts_i.at[1 + g, PARTS[h]], own_s.at[0], own_r.at[m], right)

    def hop(w, g, e, part, last=False):
        rs(w, g, e + 1, part).wait_recv()
        d, rows = NZ - e if g == 0 else e, piece(1 - w, part)
        buf, came = terms[w], (rins, lins)[g][w]
        buf[d, rows] = (buf[d, rows].astype(F32) + came[e, rows].astype(F32)).astype(BF16)
        rs(w, g, e, part, last).start()

    def end_src(w, part):
        return dwo_v.at[part_rows(part)] if w == 0 else term_i.at[0, part_rows(part)]

    def end_dst(w, rows):
        return parts_o.at[rows] if w == 0 else parts_i.at[0, rows]

    def end_copy(w, part):
        m = 2 * w + part
        return rc(end_src(w, part), end_dst(w, here), own_s.at[m], own_r.at[2 * w + b], dev(z, t2, part, a))

    def end_local(w):
        return pltpu.make_async_copy(end_src(w, a), end_dst(w, here), own_s.at[2 * w + a])

    def end_in(w, h):
        return rc(end_src(w, h), end_dst(w, PARTS[h]), own_s.at[0], own_r.at[2 * w + h], right)

    def send_own(w):
        @pl.when(same)
        def _():
            end_local(w).start()

        @pl.when(differ)
        def _():
            end_copy(w, a).start()

    def send_sum():
        rows = part_rows(1 - a)
        for g in range(2):
            rs(1, g, 1, 1 - a).wait_recv()
        total = term_i[0, rows].astype(F32)
        for came in (rin_i, lin_i):
            total = total + came[0, rows].astype(F32)
        term_i[0, rows] = total.astype(BF16)
        end_copy(1, 1 - a).start()

    def wait_end(w):
        @pl.when(same)
        def _():
            end_local(w).wait()
            if w == 1:
                for g in range(2):
                    for h in range(2):
                        last_in(1, g, h).wait_recv()

        @pl.when(differ)
        def _():
            end_copy(w, a).wait_send()

        end_copy(w, 1 - a).wait_send()
        for h in range(2):
            @pl.when(jnp.logical_not(same & (b == h)))
            def _():
                end_in(w, h).wait_recv()

    step(0, 1, a)
    step(0, 1, 1 - a)
    for r in (1, 2, 3):
        from_source(r, far_y_in(r).wait_recv)
    for r in (1, 3, 2):
        far_x(r).start()
    for i in range(2):
        ex_y(i).start()

    @pl.when(same)
    def _():
        to_twin(1).start()

    @pl.when(differ)
    def _():
        for h in range(2):
            to_chip(1, h).start()

    step(0, 2, a)
    step(0, 2, 1 - a)
    pass_on(0)

    @pl.when(same)
    def _():
        for r in (1, 2, 3):
            near_x_in(r).wait_recv()
        for r in (1, 3, 2):
            near_y(r).start()

    @pl.when(same)
    def _():
        ld_w(1).wait()

    @pl.when(differ)
    def _():
        from_twin(1).wait_recv()

    from_chip(1).wait_recv()
    wo_cp = rc(wo.at[b], wo.at[b], core_s.at[1], core_r.at[1], other_core)
    wo_in = rc(wo.at[1 - b], wo.at[1 - b], core_s.at[1], core_r.at[1], other_core)
    wo_cp.start()
    for g in range(2):
        ag(0, g, 3, firsts[g]).wait_recv()
        ag(0, g, 4, firsts[g]).start()
    pass_on(1)
    wo_in.wait_recv()
    for r in (1, 2, 3):
        far_x_in(r).wait_recv()
    make_terms(0, 0, 3)
    for g in range(2):
        rs(0, g, 4, firsts[g]).start()
    for g in range(2):
        rs(0, g, 3, seconds[g]).start()
    for g in range(2):
        hop(0, g, 3, firsts[g])
    for r in (1, 2, 3):
        ex_x_in(0, r).wait_recv()
    accumulate(pre, xt, wi, (0,), True)
    accumulate(pre, xt, wi, (1, 7))
    accumulate(pre, xt, wi, (2,))
    for r in (1, 2, 3):
        from_source(r, near_y_in(r).wait_recv)
    make_terms(0, 3, 5)
    for g in range(2):
        hop(0, g, 2, seconds[g])
    for g in range(2):
        ag(0, g, 3, seconds[g]).wait_recv()
    for r in (1, 2, 3):
        ex_x_in(1, r).wait_recv()
    accumulate(pre, xt, wi, (6,))
    accumulate(pre, xt, wi, (3, 5))
    for g in range(2):
        ag(0, g, 4, firsts[g]).wait_recv()
    accumulate(pre, xt, wi, (4,))
    pre_cp = rc(pre.at[1 - b], pre_in, core_s.at[0], core_r.at[0], other_core)
    pre_cp.start()
    for g in range(2):
        hop(0, g, 2, firsts[g])
    bias_cp.wait_recv()
    bias = jnp.where(same, bias_in[0], bias_in[1])[0:1]
    pre_cp.wait_recv()

    def gelu(i, carry):
        rows = pl.ds(pl.multiple_of(i * 32, 32), 32)
        v = pre[b, rows] + pre_in[rows] + bias
        cdf = 0.5 * (1.0 + lax.erf(v * ROOT_HALF))
        act[0, rows] = (v * cdf).astype(BF16)
        slope[rows] = cdf + v * jnp.exp(-0.5 * v * v) * INV_ROOT_TWO_PI
        return carry

    lax.fori_loop(0, 8, gelu, 0)

    for pick in (firsts, seconds):
        for g in range(2):
            ag(1, g, 1, pick[g]).start()
    make_terms(0, 5, 8)

    def add_out(slots, first=False):
        n = len(slots)

        def body(i, carry):
            q, h = lax.div(i, 2), lax.rem(i, 2)
            d = slots[0] if n == 1 else slots[0] + q * (slots[1] - slots[0])
            j = (slots[0] + 2) % NZ if n == 1 else lax.rem(d + 2, NZ)
            dwo[h] += dot(dyt[j, h].reshape(SH, ROWS), act[d], NN)
            return carry

        if first:
            dwo[...] = jnp.zeros_like(dwo)
        lax.fori_loop(0, 2 * n, body, 0)

    def pass_act(s, picks):
        for pick in picks:
            for g in range(2):
                ag(1, g, s, pick[g]).wait_recv()
                ag(1, g, s + 1, pick[g]).start()

    pass_act(1, (firsts, seconds))
    for pick in (seconds, firsts):
        for g in range(2):
            hop(0, g, 1, pick[g])
    add_out((0,), True)
    add_out((1, 7))
    pass_act(2, (firsts, seconds))
    add_out((2, 6))
    for pick in (seconds, firsts):
        for g in range(2):
            rs(0, g, 1, pick[g]).wait_recv()

    def grad(i, carry):
        rows = pl.ds(pl.multiple_of(i * 32, 32), 32)
        v = term_g[0, rows].astype(F32) + rin_g[0, rows].astype(F32) + lin_g[0, rows].astype(F32)
        gp[b, rows] = (v * slope[rows]).astype(BF16)
        return carry

    lax.fori_loop(0, 8, grad, 0)
    gp_cp = rc(gp.at[b], gp.at[b], core_s.at[4], core_r.at[4], other_core)
    gp_cp.start()
    rc(gp.at[1 - b], gp.at[1 - b], core_s.at[4], core_r.at[4], other_core).wait_recv()
    make_terms(1, 0, 3)
    for g in range(2):
        rs(1, g, 4, firsts[g]).start()
    for g in range(2):
        rs(1, g, 3, seconds[g]).start()

    def dx_body(i, carry):
        k, h = lax.div(i, 2), lax.rem(i, 2)
        d = lax.rem(z + NZ - k, NZ)
        v = dot(wi[d], gp[h], NT_DIMS).astype(BF16)
        xx, yy = lax.div(k, 2), 2 * lax.rem(k, 2) + h
        dxa[xx, yy] = v[:HF]
        dxb[yy, xx] = v[HF:]
        return carry

    lax.fori_loop(0, 16, dx_body, 0)
    yy_ = 2 * ypar + a

    def y_index(r):
        yl, ah = y_peer(r)
        return 2 * yl + ah

    def first_a(r):
        return rc(dxa.at[x_peer(r)], in_a.at[r - 1], dx_s.at[r - 1], dx_r.at[r - 1], x_dev(r))

    def first_b(r):
        return rc(dxb.at[y_index(r)], in_b.at[r - 1], dx_s.at[r + 2], dx_r.at[r + 2], y_dev(r))

    def second_a(r):
        return rc(sum_a.at[y_index(r)], last_a.at[r - 1], dx_s.at[r + 5], dx_r.at[r + 5], y_dev(r))

    def second_b(r):
        return rc(sum_b.at[x_peer(r)], last_b.at[r - 1], dx_s.at[r + 8], dx_r.at[r + 8], x_dev(r))

    for r in (1, 2, 3):
        first_a(r).start()
        first_b(r).start()

    for g in range(2):
        hop(1, g, 3, firsts[g])
    pass_act(3, (firsts,))
    make_terms(1, 3, 8)
    send_own(1)
    for part in (1 - a, a):
        for g in range(2):
            hop(1, g, 2, part)

    for g in range(2):
        ag(1, g, 3, seconds[g]).wait_recv()
    add_out((3, 5))
    for g in range(2):
        ag(1, g, 4, firsts[g]).wait_recv()
    add_out((4,))
    dwo_cp = rc(dwo.at[1 - b], dwo_in, core_s.at[5], core_r.at[5], other_core)
    dwo_cp.start()
    for g in range(2):
        hop(1, g, 1, 1 - a)
    dwo_cp.wait_recv()
    dwo_v[...] = ((dwo[b] + dwo_in[...]) * scale).astype(BF16)
    send_own(0)
    end_copy(0, 1 - a).start()

    for r in (1, 2, 3):
        first_a(r).wait_recv()
        first_b(r).wait_recv()

    def sum_body(i, carry):
        total_a, total_b = dxa[x_, i].astype(F32), dxb[yy_, i].astype(F32)
        for r in range(3):
            total_a = total_a + in_a[r, i].astype(F32)
            total_b = total_b + in_b[r, i].astype(F32)
        sum_a[i], sum_b[i] = total_a.astype(BF16), total_b.astype(BF16)
        return carry

    lax.fori_loop(0, 4, sum_body, 0)
    for r in (1, 2, 3):
        second_a(r).start()
        second_b(r).start()

    for g in range(2):
        hop(1, g, 1, a, True)
    send_sum()

    for r in (1, 2, 3):
        second_a(r).wait_recv()
        second_b(r).wait_recv()
    total_a, total_b = sum_a[yy_].astype(F32), sum_b[x_].astype(F32)
    for r in range(3):
        total_a = total_a + last_a[r].astype(F32)
        total_b = total_b + last_b[r].astype(F32)
    total_a, total_b = total_a.astype(BF16), total_b.astype(BF16)
    dx_v[here] = jnp.where(b == 0, total_a, total_b)
    turn_v[...] = jnp.where(b == 0, total_b, total_a)
    dx_cp = rc(turn_v, dx_v.at[here], core_s.at[3], core_r.at[3], other_core)
    dx_cp.start()

    rc(turn_v, dx_v.at[part_rows(1 - b)], core_s.at[3], core_r.at[3], other_core).wait_recv()
    put_dx.start()


    @pl.when(same)
    def _():
        to_twin(0).wait_send()
        to_twin(1).wait_send()

    @pl.when(differ)
    def _():
        for w in range(2):
            for h in range(2):
                to_chip(w, h).wait_send()

    for w in range(2):
        for g in range(2):
            for s in (1, 2, 3):
                for part in range(2):
                    ag(w, g, s, part).wait_send()
            ag(w, g, 4, firsts[g]).wait_send()
    for i in range(2):
        ex_y(i).wait_send()
        for r in (1, 2, 3):
            ex_x(i, r).wait_send()
    for r in (1, 2, 3):
        far_x(r).wait_send()

    @pl.when(same)
    def _():
        for d in range(1, NZ):
            dy_z(d).wait_send()
        for r in (1, 2, 3):
            far_y(r).wait_send()
            near_x(r).wait_send()
            near_y(r).wait_send()

    for cp in (bias_cp, pre_cp, wo_cp, gp_cp, dwo_cp):
        cp.wait_send()
    for w in range(2):
        for g in range(2):
            rs(w, g, 4, firsts[g]).wait_send()
            for e in (3, 2) if w else (3, 2, 1):
                for part in range(2):
                    rs(w, g, e, part).wait_send()
    for r in (1, 2, 3):
        for cp in (first_a(r), first_b(r), second_a(r), second_b(r)):
            cp.wait_send()

    wait_end(0)
    wait_end(1)
    for g in range(2):
        for part in range(2):
            rs(1, g, 1, part).wait_send()
    dx_cp.wait_send()
    put_dx.wait()


def finish(dx_ref, in_ref, out_ref, dx_out, dwin_out, dwout_out):
    dx_out[...] = dx_ref[...]
    whole = lax.rem(lax.axis_index("dp"), 2) != lax.rem(lax.axis_index("tensor"), 2)
    dwout_out[...] = out_ref[...].astype(F32)

    @pl.when(whole)
    def _():
        dwin_out[...] = in_ref[0].astype(F32)

    @pl.when(jnp.logical_not(whole))
    def _():
        dwin_out[...] = in_ref[0].astype(F32) + in_ref[1].astype(F32) + in_ref[2].astype(F32)


def per_device(inputs, upstream, w_in, bias_in, w_out):
    rows, width = inputs.shape
    scale = 1.0 / math.sqrt(rows * lax.axis_size("dp"))
    any_space = pl.BlockSpec(memory_space=pl.ANY)
    vmem = pl.BlockSpec(memory_space=pltpu.VMEM)
    shard = (SH, FC)
    ring = (NZ,) + shard
    acc = (2, ROWS, FC)
    half = (ROWS, FC)
    turned = (NZ, 2, SH, ROWS)
    dx, parts_i, parts_o = pl.pallas_call(
        lambda *refs: kernel(scale, *refs),
        out_shape=(
            jax.ShapeDtypeStruct((SH, ROWS), BF16),
            jax.ShapeDtypeStruct((3,) + shard, BF16),
            jax.ShapeDtypeStruct(shard, BF16),
        ),
        in_specs=[any_space, any_space, any_space, any_space, vmem],
        out_specs=(any_space, any_space, any_space),
        scratch_shapes=[
            pltpu.VMEM((SH, ROWS), BF16),
            pltpu.VMEM((rows, width), BF16),
            pltpu.VMEM((rows, width), BF16),
            pltpu.VMEM((NZ, 2 * SH, ROWS), BF16),
            pltpu.VMEM(turned, BF16),
            pltpu.VMEM((NZ, 2, 2, 2, QD, ROWS), BF16),
            pltpu.VMEM(ring, BF16),
            pltpu.VMEM((2,) + shard, BF16),
            pltpu.VMEM(acc, F32),
            pltpu.VMEM(half, F32),
            pltpu.VMEM((NZ,) + half, BF16),
            pltpu.VMEM(acc, BF16),
            pltpu.VMEM(half, F32),
            pltpu.VMEM((NZ,) + half, BF16),
            pltpu.VMEM(ring, BF16),
            pltpu.VMEM((4,) + half, BF16),
            pltpu.VMEM((4,) + shard, BF16),
            pltpu.VMEM((4,) + half, BF16),
            pltpu.VMEM((4,) + shard, BF16),
            pltpu.VMEM((2,) + shard, F32),
            pltpu.VMEM(shard, F32),
            pltpu.VMEM(shard, BF16),
            pltpu.VMEM((4, 4, HF, ROWS), BF16),
            pltpu.VMEM((4, 4, HF, ROWS), BF16),
            pltpu.VMEM((4, HF, ROWS), BF16),
            pltpu.VMEM((4, HF, ROWS), BF16),
            pltpu.VMEM((3, 4, HF, ROWS), BF16),
            pltpu.VMEM((3, 4, HF, ROWS), BF16),
            pltpu.VMEM((3, HF, ROWS), BF16),
            pltpu.VMEM((3, HF, ROWS), BF16),
            pltpu.VMEM((HF, ROWS), BF16),
            pltpu.VMEM((2, 8, FC), F32),
            pltpu.SemaphoreType.DMA((5,)),
            pltpu.SemaphoreType.DMA((4,)),
            pltpu.SemaphoreType.DMA((4,)),
            pltpu.SemaphoreType.DMA((32,)),
            pltpu.SemaphoreType.DMA((32,)),
            pltpu.SemaphoreType.DMA((16,)),
            pltpu.SemaphoreType.DMA((16,)),
            pltpu.SemaphoreType.DMA((6,)),
            pltpu.SemaphoreType.DMA((6,)),
            pltpu.SemaphoreType.DMA((32,)),
            pltpu.SemaphoreType.DMA((32,)),
            pltpu.SemaphoreType.DMA((4,)),
            pltpu.SemaphoreType.DMA((12,)),
            pltpu.SemaphoreType.DMA((12,)),
            pltpu.SemaphoreType.DMA((12,)),
            pltpu.SemaphoreType.DMA((8,)),
            pltpu.SemaphoreType.DMA((8,)),
            pltpu.SemaphoreType.DMA((12,)),
            pltpu.SemaphoreType.DMA((12,)),
        ],
        compiler_params=pltpu.CompilerParams(
            collective_id=0, has_side_effects=True, vmem_limit_bytes=60 * 1024 * 1024
        ),
    )(inputs, upstream, w_in, w_out.T, bias_in)
    steps = 2
    part_spec = pl.BlockSpec((3, SH // steps, FC), lambda i: (0, i, 0))
    dx_spec = pl.BlockSpec((SH // steps, ROWS), lambda i: (i, 0))
    dw_spec = pl.BlockSpec((SH // steps, FC), lambda i: (i, 0))
    dx, dwin, dwout = pl.pallas_call(
        finish,
        grid=(steps,),
        out_shape=(
            jax.ShapeDtypeStruct((SH, ROWS), BF16),
            jax.ShapeDtypeStruct(shard, F32),
            jax.ShapeDtypeStruct(shard, F32),
        ),
        in_specs=[dx_spec, part_spec, dw_spec],
        out_specs=(dx_spec, dw_spec, dw_spec),
    )(dx, parts_i, parts_o)
    return dx.T, dwin, dwout.T


def solution(mesh):
    placed = (P("dp", None), P("dp", None), P("dp", "tensor"), P("tensor"), P("tensor", "dp"))
    return jax.shard_map(
        per_device,
        mesh=mesh,
        in_specs=placed,
        out_specs=(P("dp", "tensor"), P("dp", "tensor"), P("tensor", "dp")),
        check_vma=False,
    )
```

```python
import functools
import math

import jax
import jax.numpy as jnp
from jax import lax
from jax.experimental import pallas as pl
from jax.experimental.pallas import tpu as pltpu
from jax.sharding import PartitionSpec as P

MESH = pl.DeviceIdType.MESH
ROOT_HALF = 0.7071067811865476
INV_ROOT_TWO_PI = 0.3989422804014327
BF16 = jnp.bfloat16
F32 = jnp.float32

NZ = 8
NT = 8
ROWS = 256
SH = 320
HF = SH // 2
QD = SH // 4
QR = ROWS // 2
FC = 640
PARTS = (pl.ds(0, HF), pl.ds(HF, HF))

TN = (((0,), (0,)), ((), ()))
NN = (((1,), (0,)), ((), ()))
NT_DIMS = (((1,), (1,)), ((), ()))


def dot(lhs, rhs, dims):
    return lax.dot_general(lhs, rhs, dims, preferred_element_type=F32)


def kernel(
    scale, x_hbm, dy_hbm, win_hbm, wout_hbm, bias_ref,
    dx_out, parts_i, parts_o,
    dx_v, xv, dyv, tv, xt, dyt, wi, wo,
    pre, pre_in, act, gp, slope,
    term_g, term_i, rin_g, rin_i, lin_g, lin_i, dwo, dwo_in, dwo_v,
    dxa, dxb, sum_a, sum_b, in_a, in_b, last_a, last_b, turn_v, bias_in,
    ld_sem, sw_s, sw_r, ag_s, ag_r, ex_s, ex_r, core_s, core_r,
    rs_s, rs_r, own_s, own_r, dx_s, dx_r, dz_s, dz_r, dy_s, dy_r,
):
    dp = lax.axis_index("dp")
    tn = lax.axis_index("tensor")
    z, a = lax.div(dp, 2), lax.rem(dp, 2)
    t2, b = lax.div(tn, 2), lax.rem(tn, 2)
    x_, ypar = lax.div(t2, 2), lax.rem(t2, 2)
    y_ = 2 * a + ypar
    same = a == b
    differ = a != b
    zr, zl = lax.rem(z + 1, NZ), lax.rem(z + NZ - 1, NZ)

    def dev(z_, t_, a_, b_):
        return {"dp": 2 * z_ + a_, "tensor": 2 * t_ + b_}

    right, left = dev(zr, t2, a, b), dev(zl, t2, a, b)
    other_core = dev(z, t2, a, 1 - b)
    y_side = dev(z, t2 + 1 - 2 * ypar, 1 - a, b)

    def x_peer(r):
        return lax.rem(x_ + r, 4)

    def y_peer(r):
        yy = lax.rem(y_ + r, 4)
        return lax.rem(yy, 2), lax.div(yy, 2)

    def x_dev(r):
        return dev(z, 2 * x_peer(r) + ypar, a, b)

    def y_dev(r):
        yl, ah = y_peer(r)
        return dev(z, 2 * x_ + yl, ah, b)

    def rc(src, dst, ss, rs, to):
        return pltpu.make_async_remote_copy(
            src_ref=src, dst_ref=dst, send_sem=ss, recv_sem=rs, device_id=to, device_id_type=MESH
        )

    def part_rows(p):
        if isinstance(p, int):
            return PARTS[p]
        return pl.ds(pl.multiple_of(p * HF, HF), HF)

    hbm = (win_hbm, wout_hbm)
    weights = (wi, wo)
    here = part_rows(b)

    def ld_w(w):
        return pltpu.make_async_copy(hbm[w].at[here], weights[w].at[(0, b)[w], part_rows(a)], ld_sem.at[2 + w])

    ld_x = pltpu.make_async_copy(x_hbm, xv, ld_sem.at[0])
    ld_dy = pltpu.make_async_copy(dy_hbm, dyv, ld_sem.at[1])
    put_dx = pltpu.make_async_copy(dx_v, dx_out, ld_sem.at[4])

    @pl.when(same)
    def _():
        ld_w(0).start()
        ld_w(1).start()

    pl.when(same)(ld_dy.start)
    ld_x.start()

    barrier = pltpu.get_barrier_semaphore()

    def greet(to):
        pl.semaphore_signal(barrier, inc=1, device_id=to, device_id_type=MESH)

    for z_ in (zr, zl):
        greet(dev(z_, t2, a, b))
        greet(dev(z_, t2, a, 1 - b))
    for d in range(2, 7):
        greet(dev(lax.rem(z + d, NZ), t2, a, b))
    greet(other_core)
    greet(dev(z, t2, 1 - a, b))
    greet(dev(z, t2, 1 - a, 1 - b))
    for r in (1, 2, 3):
        greet(x_dev(r))
    greet(y_dev(1))
    greet(y_dev(3))
    pl.semaphore_wait(barrier, 17)

    def to_twin(w):
        rows = part_rows(a)
        return rc(hbm[w].at[part_rows(1 - b)], weights[w].at[(0, 1 - b)[w], rows], sw_s.at[2 * w], sw_r.at[2 * w], other_core)

    def to_chip(w, h):
        rows = part_rows(a)
        return rc(
            hbm[w].at[part_rows(h)], weights[w].at[(0, h)[w], rows], sw_s.at[2 * w + h], sw_r.at[2 * w + 1], dev(z, t2, b, h)
        )

    def from_twin(w):
        return rc(hbm[w].at[here], weights[w].at[(0, b)[w], part_rows(a)], sw_s.at[2 * w], sw_r.at[2 * w], other_core)

    def from_chip(w):
        return rc(hbm[w].at[here], weights[w].at[(0, b)[w], part_rows(1 - a)], sw_s.at[2 * w], sw_r.at[2 * w + 1], other_core)

    @pl.when(same)
    def _():
        to_twin(0).start()

    @pl.when(differ)
    def _():
        for h in range(2):
            to_chip(0, h).start()

    gathered = (wi, act)

    def piece(w, part):
        size = (HF, QR)[w]
        if isinstance(part, int):
            return pl.ds(part * size, size)
        return pl.ds(pl.multiple_of(part * size, size), size)

    def ag(w, g, s, part):
        buf, rows = gathered[w], piece(w, part)
        if g == 0:
            src, dst, to = s - 1, s, right
        else:
            src, dst, to = (NZ + 1 - s) % NZ, NZ - s, left
        i = ((w * 2 + g) * 4 + s - 1) * 2 + part
        return rc(buf.at[src, rows], buf.at[dst, rows], ag_s.at[i], ag_r.at[i], to)

    def send_first(part):
        for g in range(2):
            ag(0, g, 1, part).start()

    @pl.when(same)
    def _():
        ld_w(0).wait()

    @pl.when(differ)
    def _():
        from_twin(0).wait_recv()

    send_first(a)

    xh, xq = lax.div(x_, 2), lax.rem(x_, 2)
    cut_rows = pl.ds(pl.multiple_of(SH * xq + HF * xh + QD * ypar, QD), QD)
    FAR, NEAR = pl.ds(4, 4), pl.ds(0, 4)

    def dy_z(d):
        to = dev(lax.rem(z + d, NZ), t2, a, b)
        return rc(tv.at[d, cut_rows], dyt.at[(d + 2) % NZ, xh, xq, ypar], dz_s.at[d], dz_r.at[d], to)

    def dy_msg(kind, r, batch, tail, to):
        m = kind * 3 + r - 1
        ref = dyt.at[(batch,) + tail]
        return rc(ref, ref, dy_s.at[m], dy_r.at[m], to)

    def far_y(r):
        return dy_msg(0, r, FAR, (xh, xq, ypar), y_dev(r))

    def far_y_in(r):
        return dy_msg(0, r, FAR, (xh, xq, lax.rem(y_ + 4 - r, 2)), y_dev(r))

    def far_x(r):
        return dy_msg(1, r, FAR, (xh, xq), x_dev(r))

    def far_x_in(r):
        xs = lax.rem(x_ + 4 - r, 4)
        return dy_msg(1, r, FAR, (lax.div(xs, 2), lax.rem(xs, 2)), x_dev(r))

    def near_x(r):
        return dy_msg(2, r, NEAR, (xh, xq, ypar), x_dev(r))

    def near_x_in(r):
        xs = lax.rem(x_ + 4 - r, 4)
        return dy_msg(2, r, NEAR, (lax.div(xs, 2), lax.rem(xs, 2), ypar), x_dev(r))

    whole = pl.ds(0, 2)

    def near_y(r):
        return dy_msg(3, r, NEAR, (whole, whole, ypar), y_dev(r))

    def near_y_in(r):
        return dy_msg(3, r, NEAR, (whole, whole, lax.rem(y_ + 4 - r, 2)), y_dev(r))

    def from_source(r, wait):
        pl.when(lax.div(lax.rem(y_ + 4 - r, 4), 2) == b)(wait)

    @pl.when(same)
    def _():
        ld_dy.wait()

        def turn_dy(d, carry):
            k = lax.rem(z + d, NZ)
            tv[d] = dyv[:, pl.ds(pl.multiple_of(k * 2 * SH, 128), 2 * SH)].T
            return carry

        lax.fori_loop(0, NZ, turn_dy, 0)
        for d in (4, 3, 5, 2, 6, 1, 7):
            dy_z(d).start()
        dyt[2, xh, xq, ypar] = tv[0, cut_rows]

    bias_in[0] = jnp.broadcast_to(bias_ref[...].astype(F32)[None, :], (8, FC))
    bias_cp = rc(bias_in.at[0], bias_in.at[1], core_s.at[2], core_r.at[2], other_core)
    bias_cp.start()

    quads = ((0, 1, 7, 2), (6, 3, 5, 4))

    def at_x(i, x):
        p, q, r, t = quads[i]
        return jnp.where(x < 2, jnp.where(x == 0, p, q), jnp.where(x == 2, r, t))

    def turn(src, dst, d):
        k = lax.rem(z + NZ - d, NZ)
        v = src[:, pl.ds(pl.multiple_of(k * 2 * SH, 128), 2 * SH)].T
        first = b == 0
        dst[d, a, PARTS[0]] = jnp.where(first, v[:HF], v[HF:SH])
        dst[d, a, PARTS[1]] = jnp.where(first, v[SH : SH + HF], v[SH + HF :])

    def ex_y(i):
        ref = xt.at[at_x(i, x_), a]
        return rc(ref, ref, ex_s.at[i], ex_r.at[i], y_side)

    def ex_y_in(i):
        ref = xt.at[at_x(i, x_), 1 - a]
        return rc(ref, ref, ex_s.at[i], ex_r.at[i], y_side)

    def ex_x(i, r):
        ref, m = xt.at[at_x(i, x_), 1 - a], 1 + 3 * i + r
        return rc(ref, ref, ex_s.at[m], ex_r.at[m], x_dev(r))

    def ex_x_in(i, r):
        ref, m = xt.at[at_x(i, lax.rem(x_ + 4 - r, 4)), 1 - a], 1 + 3 * i + r
        return rc(ref, ref, ex_s.at[m], ex_r.at[m], x_dev(r))

    ld_x.wait()
    for d in range(NZ):
        turn(xv, xt, d)

    from_chip(0).wait_recv()
    send_first(1 - a)

    @pl.when(same)
    def _():
        for d in (4, 3, 5, 2):
            dy_z(d).wait_recv()
        for r in (1, 3, 2):
            far_y(r).start()
        for d in (6, 1, 7):
            dy_z(d).wait_recv()
        for r in (1, 3, 2):
            near_x(r).start()

    def pass_on(i):
        ex_y_in(i).wait_recv()
        for r in (1, 3, 2):
            ex_x(i, r).start()

    def step(w, s, part):
        for g in range(2):
            ag(w, g, s, part).wait_recv()
            ag(w, g, s + 1, part).start()

    def accumulate(acc, src, w, slots, first=False):
        n = len(slots)

        def body(i, carry):
            j, h = lax.div(i, 2), lax.rem(i, 2)
            d = slots[0] if n == 1 else slots[0] + j * (slots[1] - slots[0])
            acc[h] += dot(src[d, h], w[d], TN)
            return carry

        if first:
            acc[...] = jnp.zeros_like(acc)
        lax.fori_loop(0, 2 * n, body, 0)

    firsts = (0, 1)
    seconds = (1, 0)

    terms, rins, lins = (term_g, term_i), (rin_g, rin_i), (lin_g, lin_i)

    def make_terms(w, lo, hi):
        def body(i, carry):
            d = lax.rem(4 + lax.div(i + 1, 2) * (2 * lax.rem(i, 2) - 1) + NZ, NZ)
            if w == 0:
                j = lax.rem(d + 2, NZ)
                total = dot(dyt[j, 0].reshape(SH, ROWS), wo[0], TN) + dot(dyt[j, 1].reshape(SH, ROWS), wo[1], TN)
            else:
                total = (dot(xt[d, 0], gp[0], NN) + dot(xt[d, 1], gp[1], NN)) * scale
            terms[w][d] = total.astype(BF16)
            return carry

        lax.fori_loop(lo, hi, body, 0)

    def rs(w, g, e, part, last=False):
        rows = piece(1 - w, part)
        src = terms[w].at[NZ - e if g == 0 else e, rows]
        i = ((w * 2 + g) * 4 + e - 1) * 2 + part
        if last:
            m = 4 + (w * 2 + g) * 2 + b
            return rc(src, parts_i.at[1 + g, here], rs_s.at[i], own_r.at[m], dev((zr, zl)[g], t2, a, a))
        return rc(src, (rins, lins)[g][w].at[e - 1, rows], rs_s.at[i], rs_r.at[i], (right, left)[g])

    def last_in(w, g, h):
        m = 4 + (w * 2 + g) * 2 + h
        return rc(terms[w].at[0, PARTS[h]], parts_i.at[1 + g, PARTS[h]], own_s.at[0], own_r.at[m], right)

    def hop(w, g, e, part, last=False):
        rs(w, g, e + 1, part).wait_recv()
        d, rows = NZ - e if g == 0 else e, piece(1 - w, part)
        buf, came = terms[w], (rins, lins)[g][w]
        buf[d, rows] = (buf[d, rows].astype(F32) + came[e, rows].astype(F32)).astype(BF16)
        rs(w, g, e, part, last).start()

    def end_src(w, part):
        return dwo_v.at[part_rows(part)] if w == 0 else term_i.at[0, part_rows(part)]

    def end_dst(w, rows):
        return parts_o.at[rows] if w == 0 else parts_i.at[0, rows]

    def end_copy(w, part):
        m = 2 * w + part
        return rc(end_src(w, part), end_dst(w, here), own_s.at[m], own_r.at[2 * w + b], dev(z, t2, part, a))

    def end_local(w):
        return pltpu.make_async_copy(end_src(w, a), end_dst(w, here), own_s.at[2 * w + a])

    def end_in(w, h):
        return rc(end_src(w, h), end_dst(w, PARTS[h]), own_s.at[0], own_r.at[2 * w + h], right)

    def send_own(w):
        @pl.when(same)
        def _():
            end_local(w).start()

        @pl.when(differ)
        def _():
            end_copy(w, a).start()

    def send_sum():
        rows = part_rows(1 - a)
        for g in range(2):
            rs(1, g, 1, 1 - a).wait_recv()
        total = term_i[0, rows].astype(F32)
        for came in (rin_i, lin_i):
            total = total + came[0, rows].astype(F32)
        term_i[0, rows] = total.astype(BF16)
        end_copy(1, 1 - a).start()

    def wait_end(w):
        @pl.when(same)
        def _():
            end_local(w).wait()
            if w == 1:
                for g in range(2):
                    for h in range(2):
                        last_in(1, g, h).wait_recv()

        @pl.when(differ)
        def _():
            end_copy(w, a).wait_send()

        end_copy(w, 1 - a).wait_send()
        for h in range(2):
            @pl.when(jnp.logical_not(same & (b == h)))
            def _():
                end_in(w, h).wait_recv()

    step(0, 1, a)
    step(0, 1, 1 - a)
    for r in (1, 2, 3):
        from_source(r, far_y_in(r).wait_recv)
    for r in (1, 3, 2):
        far_x(r).start()
    for i in range(2):
        ex_y(i).start()

    @pl.when(same)
    def _():
        to_twin(1).start()

    @pl.when(differ)
    def _():
        for h in range(2):
            to_chip(1, h).start()

    step(0, 2, a)
    step(0, 2, 1 - a)
    pass_on(0)

    @pl.when(same)
    def _():
        for r in (1, 2, 3):
            near_x_in(r).wait_recv()
        for r in (1, 3, 2):
            near_y(r).start()

    @pl.when(same)
    def _():
        ld_w(1).wait()

    @pl.when(differ)
    def _():
        from_twin(1).wait_recv()

    from_chip(1).wait_recv()
    wo_cp = rc(wo.at[b], wo.at[b], core_s.at[1], core_r.at[1], other_core)
    wo_in = rc(wo.at[1 - b], wo.at[1 - b], core_s.at[1], core_r.at[1], other_core)
    wo_cp.start()

    def fourth(g):
        ag(0, g, 3, firsts[g]).wait_recv()
        ag(0, g, 4, firsts[g]).start()

    for g in range(2):
        pl.when(a == g)(functools.partial(fourth, g))
    for g in range(2):
        pl.when(a != g)(functools.partial(fourth, g))
    pass_on(1)
    wo_in.wait_recv()
    for r in (1, 2, 3):
        far_x_in(r).wait_recv()
    make_terms(0, 0, 3)
    for g in range(2):
        rs(0, g, 4, firsts[g]).start()
    for g in range(2):
        rs(0, g, 3, seconds[g]).start()
    for g in range(2):
        hop(0, g, 3, firsts[g])
    for r in (1, 2, 3):
        ex_x_in(0, r).wait_recv()
    accumulate(pre, xt, wi, (0,), True)
    accumulate(pre, xt, wi, (1, 7))
    accumulate(pre, xt, wi, (2,))
    for r in (1, 2, 3):
        from_source(r, near_y_in(r).wait_recv)
    make_terms(0, 3, 5)
    for g in range(2):
        hop(0, g, 2, seconds[g])
    for g in range(2):
        ag(0, g, 3, seconds[g]).wait_recv()
    for r in (1, 2, 3):
        ex_x_in(1, r).wait_recv()
    accumulate(pre, xt, wi, (6,))
    accumulate(pre, xt, wi, (3, 5))
    for g in range(2):
        ag(0, g, 4, firsts[g]).wait_recv()
    accumulate(pre, xt, wi, (4,))
    pre_cp = rc(pre.at[1 - b], pre_in, core_s.at[0], core_r.at[0], other_core)
    pre_cp.start()
    for g in range(2):
        hop(0, g, 2, firsts[g])
    bias_cp.wait_recv()
    bias = jnp.where(same, bias_in[0], bias_in[1])[0:1]
    pre_cp.wait_recv()

    def gelu(i, carry):
        rows = pl.ds(pl.multiple_of(i * 32, 32), 32)
        v = pre[b, rows] + pre_in[rows] + bias
        cdf = 0.5 * (1.0 + lax.erf(v * ROOT_HALF))
        act[0, rows] = (v * cdf).astype(BF16)
        slope[rows] = cdf + v * jnp.exp(-0.5 * v * v) * INV_ROOT_TWO_PI
        return carry

    lax.fori_loop(0, 8, gelu, 0)

    for pick in (firsts, seconds):
        for g in range(2):
            ag(1, g, 1, pick[g]).start()
    make_terms(0, 5, 8)

    def add_out(slots, first=False):
        n = len(slots)

        def body(i, carry):
            q, h = lax.div(i, 2), lax.rem(i, 2)
            d = slots[0] if n == 1 else slots[0] + q * (slots[1] - slots[0])
            j = (slots[0] + 2) % NZ if n == 1 else lax.rem(d + 2, NZ)
            dwo[h] += dot(dyt[j, h].reshape(SH, ROWS), act[d], NN)
            return carry

        if first:
            dwo[...] = jnp.zeros_like(dwo)
        lax.fori_loop(0, 2 * n, body, 0)

    def pass_act(s, picks):
        for pick in picks:
            for g in range(2):
                ag(1, g, s, pick[g]).wait_recv()
                ag(1, g, s + 1, pick[g]).start()

    pass_act(1, (firsts, seconds))
    for pick in (seconds, firsts):
        for g in range(2):
            hop(0, g, 1, pick[g])
    add_out((0,), True)
    add_out((1, 7))
    pass_act(2, (firsts, seconds))
    add_out((2, 6))
    for pick in (seconds, firsts):
        for g in range(2):
            rs(0, g, 1, pick[g]).wait_recv()

    def grad(i, carry):
        rows = pl.ds(pl.multiple_of(i * 32, 32), 32)
        v = term_g[0, rows].astype(F32) + rin_g[0, rows].astype(F32) + lin_g[0, rows].astype(F32)
        gp[b, rows] = (v * slope[rows]).astype(BF16)
        return carry

    lax.fori_loop(0, 8, grad, 0)
    gp_cp = rc(gp.at[b], gp.at[b], core_s.at[4], core_r.at[4], other_core)
    gp_cp.start()
    rc(gp.at[1 - b], gp.at[1 - b], core_s.at[4], core_r.at[4], other_core).wait_recv()
    make_terms(1, 0, 3)
    for g in range(2):
        rs(1, g, 4, firsts[g]).start()
    for g in range(2):
        rs(1, g, 3, seconds[g]).start()

    def dx_body(i, carry):
        k, h = lax.div(i, 2), lax.rem(i, 2)
        d = lax.rem(z + NZ - k, NZ)
        v = dot(wi[d], gp[h], NT_DIMS).astype(BF16)
        xx, yy = lax.div(k, 2), 2 * lax.rem(k, 2) + h
        dxa[xx, yy] = v[:HF]
        dxb[yy, xx] = v[HF:]
        return carry

    lax.fori_loop(0, 16, dx_body, 0)
    yy_ = 2 * ypar + a

    def y_index(r):
        yl, ah = y_peer(r)
        return 2 * yl + ah

    def first_a(r):
        return rc(dxa.at[x_peer(r)], in_a.at[r - 1], dx_s.at[r - 1], dx_r.at[r - 1], x_dev(r))

    def first_b(r):
        return rc(dxb.at[y_index(r)], in_b.at[r - 1], dx_s.at[r + 2], dx_r.at[r + 2], y_dev(r))

    def second_a(r):
        return rc(sum_a.at[y_index(r)], last_a.at[r - 1], dx_s.at[r + 5], dx_r.at[r + 5], y_dev(r))

    def second_b(r):
        return rc(sum_b.at[x_peer(r)], last_b.at[r - 1], dx_s.at[r + 8], dx_r.at[r + 8], x_dev(r))

    for r in (1, 2, 3):
        first_a(r).start()
        first_b(r).start()

    for g in range(2):
        hop(1, g, 3, firsts[g])
    pass_act(3, (firsts,))
    make_terms(1, 3, 8)
    send_own(1)
    for part in (1 - a, a):
        for g in range(2):
            hop(1, g, 2, part)

    for g in range(2):
        ag(1, g, 3, seconds[g]).wait_recv()
    add_out((3, 5))
    for g in range(2):
        ag(1, g, 4, firsts[g]).wait_recv()
    add_out((4,))
    dwo_cp = rc(dwo.at[1 - b], dwo_in, core_s.at[5], core_r.at[5], other_core)
    dwo_cp.start()
    for g in range(2):
        hop(1, g, 1, 1 - a)
    dwo_cp.wait_recv()
    dwo_v[...] = ((dwo[b] + dwo_in[...]) * scale).astype(BF16)
    send_own(0)
    end_copy(0, 1 - a).start()

    for r in (1, 2, 3):
        first_a(r).wait_recv()
        first_b(r).wait_recv()

    def sum_body(i, carry):
        total_a, total_b = dxa[x_, i].astype(F32), dxb[yy_, i].astype(F32)
        for r in range(3):
            total_a = total_a + in_a[r, i].astype(F32)
            total_b = total_b + in_b[r, i].astype(F32)
        sum_a[i], sum_b[i] = total_a.astype(BF16), total_b.astype(BF16)
        return carry

    lax.fori_loop(0, 4, sum_body, 0)
    for r in (1, 2, 3):
        second_a(r).start()
        second_b(r).start()

    for g in range(2):
        hop(1, g, 1, a, True)
    send_sum()

    for r in (1, 2, 3):
        second_a(r).wait_recv()
        second_b(r).wait_recv()
    total_a, total_b = sum_a[yy_].astype(F32), sum_b[x_].astype(F32)
    for r in range(3):
        total_a = total_a + last_a[r].astype(F32)
        total_b = total_b + last_b[r].astype(F32)
    total_a, total_b = total_a.astype(BF16), total_b.astype(BF16)
    dx_v[here] = jnp.where(b == 0, total_a, total_b)
    turn_v[...] = jnp.where(b == 0, total_b, total_a)
    dx_cp = rc(turn_v, dx_v.at[here], core_s.at[3], core_r.at[3], other_core)
    dx_cp.start()

    rc(turn_v, dx_v.at[part_rows(1 - b)], core_s.at[3], core_r.at[3], other_core).wait_recv()
    put_dx.start()


    @pl.when(same)
    def _():
        to_twin(0).wait_send()
        to_twin(1).wait_send()

    @pl.when(differ)
    def _():
        for w in range(2):
            for h in range(2):
                to_chip(w, h).wait_send()

    for w in range(2):
        for g in range(2):
            for s in (1, 2, 3):
                for part in range(2):
                    ag(w, g, s, part).wait_send()
            ag(w, g, 4, firsts[g]).wait_send()
    for i in range(2):
        ex_y(i).wait_send()
        for r in (1, 2, 3):
            ex_x(i, r).wait_send()
    for r in (1, 2, 3):
        far_x(r).wait_send()

    @pl.when(same)
    def _():
        for d in range(1, NZ):
            dy_z(d).wait_send()
        for r in (1, 2, 3):
            far_y(r).wait_send()
            near_x(r).wait_send()
            near_y(r).wait_send()

    for cp in (bias_cp, pre_cp, wo_cp, gp_cp, dwo_cp):
        cp.wait_send()
    for w in range(2):
        for g in range(2):
            rs(w, g, 4, firsts[g]).wait_send()
            for e in (3, 2) if w else (3, 2, 1):
                for part in range(2):
                    rs(w, g, e, part).wait_send()
    for r in (1, 2, 3):
        for cp in (first_a(r), first_b(r), second_a(r), second_b(r)):
            cp.wait_send()

    wait_end(0)
    wait_end(1)
    for g in range(2):
        for part in range(2):
            rs(1, g, 1, part).wait_send()
    dx_cp.wait_send()
    put_dx.wait()


def finish(dx_ref, in_ref, out_ref, dx_out, dwin_out, dwout_out):
    dx_out[...] = dx_ref[...]
    whole = lax.rem(lax.axis_index("dp"), 2) != lax.rem(lax.axis_index("tensor"), 2)
    dwout_out[...] = out_ref[...].astype(F32)

    @pl.when(whole)
    def _():
        dwin_out[...] = in_ref[0].astype(F32)

    @pl.when(jnp.logical_not(whole))
    def _():
        dwin_out[...] = in_ref[0].astype(F32) + in_ref[1].astype(F32) + in_ref[2].astype(F32)


def per_device(inputs, upstream, w_in, bias_in, w_out):
    rows, width = inputs.shape
    scale = 1.0 / math.sqrt(rows * lax.axis_size("dp"))
    any_space = pl.BlockSpec(memory_space=pl.ANY)
    vmem = pl.BlockSpec(memory_space=pltpu.VMEM)
    shard = (SH, FC)
    ring = (NZ,) + shard
    acc = (2, ROWS, FC)
    half = (ROWS, FC)
    turned = (NZ, 2, SH, ROWS)
    dx, parts_i, parts_o = pl.pallas_call(
        lambda *refs: kernel(scale, *refs),
        out_shape=(
            jax.ShapeDtypeStruct((SH, ROWS), BF16),
            jax.ShapeDtypeStruct((3,) + shard, BF16),
            jax.ShapeDtypeStruct(shard, BF16),
        ),
        in_specs=[any_space, any_space, any_space, any_space, vmem],
        out_specs=(any_space, any_space, any_space),
        scratch_shapes=[
            pltpu.VMEM((SH, ROWS), BF16),
            pltpu.VMEM((rows, width), BF16),
            pltpu.VMEM((rows, width), BF16),
            pltpu.VMEM((NZ, 2 * SH, ROWS), BF16),
            pltpu.VMEM(turned, BF16),
            pltpu.VMEM((NZ, 2, 2, 2, QD, ROWS), BF16),
            pltpu.VMEM(ring, BF16),
            pltpu.VMEM((2,) + shard, BF16),
            pltpu.VMEM(acc, F32),
            pltpu.VMEM(half, F32),
            pltpu.VMEM((NZ,) + half, BF16),
            pltpu.VMEM(acc, BF16),
            pltpu.VMEM(half, F32),
            pltpu.VMEM((NZ,) + half, BF16),
            pltpu.VMEM(ring, BF16),
            pltpu.VMEM((4,) + half, BF16),
            pltpu.VMEM((4,) + shard, BF16),
            pltpu.VMEM((4,) + half, BF16),
            pltpu.VMEM((4,) + shard, BF16),
            pltpu.VMEM((2,) + shard, F32),
            pltpu.VMEM(shard, F32),
            pltpu.VMEM(shard, BF16),
            pltpu.VMEM((4, 4, HF, ROWS), BF16),
            pltpu.VMEM((4, 4, HF, ROWS), BF16),
            pltpu.VMEM((4, HF, ROWS), BF16),
            pltpu.VMEM((4, HF, ROWS), BF16),
            pltpu.VMEM((3, 4, HF, ROWS), BF16),
            pltpu.VMEM((3, 4, HF, ROWS), BF16),
            pltpu.VMEM((3, HF, ROWS), BF16),
            pltpu.VMEM((3, HF, ROWS), BF16),
            pltpu.VMEM((HF, ROWS), BF16),
            pltpu.VMEM((2, 8, FC), F32),
            pltpu.SemaphoreType.DMA((5,)),
            pltpu.SemaphoreType.DMA((4,)),
            pltpu.SemaphoreType.DMA((4,)),
            pltpu.SemaphoreType.DMA((32,)),
            pltpu.SemaphoreType.DMA((32,)),
            pltpu.SemaphoreType.DMA((16,)),
            pltpu.SemaphoreType.DMA((16,)),
            pltpu.SemaphoreType.DMA((6,)),
            pltpu.SemaphoreType.DMA((6,)),
            pltpu.SemaphoreType.DMA((32,)),
            pltpu.SemaphoreType.DMA((32,)),
            pltpu.SemaphoreType.DMA((4,)),
            pltpu.SemaphoreType.DMA((12,)),
            pltpu.SemaphoreType.DMA((12,)),
            pltpu.SemaphoreType.DMA((12,)),
            pltpu.SemaphoreType.DMA((8,)),
            pltpu.SemaphoreType.DMA((8,)),
            pltpu.SemaphoreType.DMA((12,)),
            pltpu.SemaphoreType.DMA((12,)),
        ],
        compiler_params=pltpu.CompilerParams(
            collective_id=0, has_side_effects=True, vmem_limit_bytes=60 * 1024 * 1024
        ),
    )(inputs, upstream, w_in, w_out.T, bias_in)
    steps = 2
    part_spec = pl.BlockSpec((3, SH // steps, FC), lambda i: (0, i, 0))
    dx_spec = pl.BlockSpec((SH // steps, ROWS), lambda i: (i, 0))
    dw_spec = pl.BlockSpec((SH // steps, FC), lambda i: (i, 0))
    dx, dwin, dwout = pl.pallas_call(
        finish,
        grid=(steps,),
        out_shape=(
            jax.ShapeDtypeStruct((SH, ROWS), BF16),
            jax.ShapeDtypeStruct(shard, F32),
            jax.ShapeDtypeStruct(shard, F32),
        ),
        in_specs=[dx_spec, part_spec, dw_spec],
        out_specs=(dx_spec, dw_spec, dw_spec),
    )(dx, parts_i, parts_o)
    return dx.T, dwin, dwout.T


def solution(mesh):
    placed = (P("dp", None), P("dp", None), P("dp", "tensor"), P("tensor"), P("tensor", "dp"))
    return jax.shard_map(
        per_device,
        mesh=mesh,
        in_specs=placed,
        out_specs=(P("dp", "tensor"), P("dp", "tensor"), P("tensor", "dp")),
        check_vma=False,
    )
```
